128 devices in a mesh: shot: 4 (over x), blk: 32 (over z, y, core).
Axes of the slice: x: 4, y: 4, z: 4, core: 2. Of those that a mesh axis runs over, the one named last changes fastest.
Arguments:
- intensities: bfloat16 [8192, 16, 128], P('blk', 'shot'), may hold values from -6 to 6
- tile_owner: int32 [8192], P('blk'), may hold values from 0 to 31, as said below
- tile_place: int32 [8192], P('blk'), may hold values from 0 to 255
- tile_kernel: int32 [8192], P('blk'), may hold values from 0 to 3
- mask_len: int32 [8192], P('blk'), may hold values from 1 to 128
- interp_weights: bfloat16 [4, 128, 128], replicated, may hold values from 0 to 1.2
Outputs:
- corr_diff: float32 [16, 512, 2048], P('shot', 'blk')
The draws below stay inside these ranges and needn't reach their ends.
Inputs may be any that keep to these rules, and one draw needn't show every extreme that they name: `tile_owner`: in each device's block of 256 tiles no owner is named by more than 24 tiles, and one owner, the same for every block, is named by exactly 24 tiles of every block.
All inputs are finite; a program needn't handle non-finite values.
Results may differ from the reference program's by a relative error of at most 0.0003.
Values may be sent and summed in bfloat16 or wider, within the bound.
A program may use at most 64 MiB of HBM per device.

```python
import math
import jax
import jax.numpy as jnp
import numpy as np
from jax import lax

ANG = 2048
TP = 128
Q_DEV = 16
KERN = 4
TILES_DEV = 256
NSEG = 16
OWNERS = 32
Q = 512
CAP = 24
TILES = 8192
SHOTS = 16


def draw_tile_owner(key, part):
    hot_owner = jax.random.randint(jax.random.fold_in(key, 11), (), 0, OWNERS)
    others = jnp.arange((OWNERS - 1) * CAP, dtype=jnp.int32) // CAP
    others = others + (others >= hot_owner).astype(jnp.int32)

    def one_block(block_key):
        first_key, second_key = jax.random.split(block_key)
        selected_index = jax.random.permutation(first_key, others)[:TILES_DEV - CAP]
        filled = jnp.concatenate([jnp.full((CAP,), hot_owner, jnp.int32), selected_index])
        return jax.random.permutation(second_key, filled)
    block_keys = jax.random.split(jax.random.fold_in(key, 13), OWNERS)
    return jax.vmap(one_block)(block_keys).reshape(-1).astype(jnp.int32)


def draw_interp_weights(key, part):
    diag_key, off_key = jax.random.split(jax.random.fold_in(key, 17))
    diagonal = jax.random.uniform(diag_key, (KERN, TP), jnp.float32, 0.5, 1.0)
    spread = jax.random.uniform(off_key, (KERN, TP, TP), jnp.float32, 0.0, 0.6 / TP)
    identity = jnp.eye(TP, dtype=jnp.float32)
    return (spread * (1.0 - identity)[None] + identity[None] * diagonal[:, None, :]).astype(jnp.bfloat16)


def set_ends(array, rng, least, largest):
    spot = [jax.random.randint(jax.random.fold_in(rng, axis), (), 0, length) for axis, length in enumerate(array.shape)]
    longest = array.shape.index(max(array.shape))
    next_to = spot[:longest] + [(spot[longest] + 1) % array.shape[longest]] + spot[longest + 1:]
    return array.at[tuple(spot)].set(least).at[tuple(next_to)].set(largest)


def shard_levels(own_key, shape, cuts, low, largest):
    level, own = 1.0, jax.random.fold_in(own_key, 6)
    for position, shards_of in cuts:
        draws = jnp.exp(jax.random.uniform(jax.random.fold_in(own, position), (shards_of,), jnp.float32, low / len(cuts), largest / len(cuts)))
        level = level * jnp.repeat(draws, shape[position] // shards_of).reshape([-1 if axis == position else 1 for axis in range(len(shape))])
    return level


def cumulative_ranks(amount, skew):
    portions = [(1 << 20) // math.isqrt(grade ** skew) + 1 for grade in range(1, amount + 1)]
    width = 1 + sum(portions) // (1 << 30)
    return np.cumsum(np.array([max(1, weight // width) for weight in portions]))


def ranked_ids(key, shape, amount, slope):
    table = cumulative_ranks(amount, slope)
    ticket = jax.random.randint(jax.random.fold_in(key, 1), shape, 0, int(table[amount - 1]))
    rank = jnp.searchsorted(jnp.asarray(table, jnp.int32), ticket, side="right")
    return jax.random.permutation(jax.random.fold_in(key, 2), amount)[rank].astype(jnp.int32)


def normal_values(key, shape, width, limit, shards=(), kind=jnp.bfloat16):
    values = width * jax.random.normal(key, shape, jnp.float32)
    if shards:
        values = values * shard_levels(key, shape, shards, -0.22, 0.18)
    return jnp.clip(values, -limit, limit).astype(kind)


def setup_inputs(seed: int = 0) -> dict:
    splits = jax.random.split(jax.random.key(seed), 7)
    intensities = normal_values(splits[0], (TILES, SHOTS, TP), 1.0, 6.0, ((0, 32), (1, 4)))
    tile_owner = draw_tile_owner(jax.random.fold_in(splits[6], 71), 0)
    tile_place = set_ends(ranked_ids(splits[2], (TILES,), Q_DEV * NSEG, 3), jax.random.fold_in(splits[2], 3), 0, (Q_DEV * NSEG) - 1).astype(jnp.int32)
    tile_kernel = set_ends(jax.random.randint(splits[3], (TILES,), 0, KERN), jax.random.fold_in(splits[3], 1), 0, KERN - 1).astype(jnp.int32)
    mask_len = set_ends(jax.random.randint(splits[4], (TILES,), 1, TP + 1), jax.random.fold_in(splits[4], 1), 1, TP).astype(jnp.int32)
    interp_weights = draw_interp_weights(jax.random.fold_in(splits[6], 71), 0)
    return {"intensities": intensities, "tile_owner": tile_owner, "tile_place": tile_place, "tile_kernel": tile_kernel, "mask_len": mask_len, "interp_weights": interp_weights}


def reference(intensities, tile_owner, tile_place, tile_kernel, mask_len, interp_weights):
    slot_count = Q_DEV * NSEG
    weights = interp_weights.astype(jnp.float32)
    pixel_index = jnp.arange(TP, dtype=jnp.int32)
    blocks = (
        intensities.reshape(OWNERS, TILES_DEV, SHOTS, TP),
        tile_owner.reshape(OWNERS, TILES_DEV),
        tile_place.reshape(OWNERS, TILES_DEV),
        tile_kernel.reshape(OWNERS, TILES_DEV),
        mask_len.reshape(OWNERS, TILES_DEV),
    )

    def block_step(running, block_data):
        pixels, owners, places, kernels, lengths = block_data
        live_values = (pixel_index[None, :] < lengths[:, None]).astype(jnp.float32)
        selected_rows = jnp.take(weights, kernels, axis=0)
        masked_intensity = pixels.astype(jnp.float32) * live_values[:, None, :]
        value_entries = jnp.einsum("tsp,tpa->tsa", masked_intensity, selected_rows, precision=lax.Precision.HIGHEST)
        mask_values = jnp.einsum("tp,tpa->ta", live_values, selected_rows, precision=lax.Precision.HIGHEST)
        slot_ids = (owners * slot_count + places).astype(jnp.int32)
        total_values = running[0] + jax.ops.segment_sum(value_entries, slot_ids, num_segments=OWNERS * slot_count)
        total_masks = running[1] + jax.ops.segment_sum(mask_values, slot_ids, num_segments=OWNERS * slot_count)
        return (total_values, total_masks), None

    start = (
        jnp.zeros((OWNERS * slot_count, SHOTS, TP), jnp.float32),
        jnp.zeros((OWNERS * slot_count, TP), jnp.float32),
    )
    finals = lax.scan(block_step, start, blocks)[0]
    cycle_int = finals[0].reshape(Q, NSEG, SHOTS, TP).transpose(2, 0, 1, 3).reshape(SHOTS, Q, ANG)
    cycle_mask = finals[1].reshape(Q, ANG)
    next_int = jnp.roll(cycle_int, -1, axis=0)
    spectrum = jnp.fft.fft(cycle_int, axis=-1)
    next_spectrum = jnp.fft.fft(next_int, axis=-1)
    auto_corr = jnp.real(jnp.fft.ifft(spectrum * jnp.conj(spectrum), axis=-1))
    cross_corr = jnp.real(jnp.fft.ifft(spectrum * jnp.conj(next_spectrum), axis=-1))
    mask_spectrum = jnp.fft.fft(cycle_mask, axis=-1)
    mask_corr = jnp.real(jnp.fft.ifft(mask_spectrum * jnp.conj(mask_spectrum), axis=-1))
    denominator = jnp.maximum(jnp.maximum(mask_corr, 0.01 * mask_corr[:, :1]), 1.0)
    return ((auto_corr - cross_corr) / denominator[None]).astype(jnp.float32)
```

```python
import functools
import math

import jax
import jax.numpy as jnp
import numpy as np
from jax import lax
from jax.experimental import pallas as pl
from jax.experimental.pallas import tpu as pltpu
from jax.sharding import PartitionSpec as P

ANG = 2048
TP = 128
Q_DEV = 16
NSEG = 16
HALF = NSEG // 2
FREQS = HALF + 1
ROWS = FREQS * Q_DEV
FIELD = 32
GROUP = 4
MESH = pl.DeviceIdType.MESH


def dft_tables():
    b = np.arange(TP)
    angle = 2.0 * math.pi * (np.outer(b, b) % TP) / TP
    cos, sin = np.cos(angle), np.sin(angle)
    table = np.block([[cos, -sin], [sin, cos]]).astype(np.float32)
    high = table.astype(jnp.bfloat16)
    low = (table - high.astype(np.float32)).astype(jnp.bfloat16)
    dft = np.concatenate([high, high, low], axis=0)
    twist = 2.0 * math.pi * (np.outer(np.arange(FREQS), b) % ANG) / ANG
    scale = np.full((FREQS, 1), 2.0 / ANG)
    scale[0] = scale[HALF] = 1.0 / ANG
    turns = np.stack(
        [np.cos(twist), -np.sin(twist), scale * np.cos(twist), -scale * np.sin(twist)]
    ).astype(np.float32)
    return dft, turns


def cosine_sums(first, middle, rest):
    c1, c3, r2 = math.cos(math.pi / 8), math.cos(3 * math.pi / 8), math.sqrt(0.5)
    even, odd = first + middle, first - middle
    g, h = rest[2] + rest[6], r2 * (rest[2] - rest[6])
    base = even + rest[4]
    p = [base + g, odd + h, even - rest[4], odd - h, base - g]
    u1, u3 = rest[1] - rest[7], rest[3] - rest[5]
    t1, t3 = rest[1] + rest[7], rest[3] + rest[5]
    q = [t1 + t3, c1 * u1 + c3 * u3, r2 * (t1 - t3), c3 * u1 - c1 * u3]
    low = [p[k] + q[k] for k in range(4)]
    high = [p[k] - q[k] for k in range(3, -1, -1)]
    return low + [p[4]] + high


def sine_sums(v):
    c1, c3, r2 = math.cos(math.pi / 8), math.cos(3 * math.pi / 8), math.sqrt(0.5)
    e = r2 * (v[2] + v[6])
    w = [None, e + v[4], v[2] - v[6], e - v[4]]
    a, b = v[1] + v[7], v[3] + v[5]
    s, t = v[1] - v[7], v[3] - v[5]
    o = [None, c3 * a + c1 * b, r2 * (s + t), c1 * a - c3 * b]
    low = [o[k] + w[k] for k in range(1, 4)]
    high = [o[k] - w[k] for k in range(3, 0, -1)]
    return [None] + low + [s - t] + high


def split(x):
    high = x.astype(jnp.bfloat16)
    return high, (x - high.astype(jnp.float32)).astype(jnp.bfloat16)


def dot(a, b, rhs_dim=0):
    return lax.dot_general(
        a, b, (((1,), (rhs_dim,)), ((), ())), preferred_element_type=jnp.float32
    )


def kernel(
    owners, cap, shots, shot_blocks,
    pix_ref, owner_ref, place_ref, kind_ref, len_ref, weights_ref, dft_ref, turns_ref,
    out_ref,
    wide, send, recv, meta, meta_send, meta_recv, place_col, kind_col, len_col,
    chosen, values, cycles, halo, high, low, spectra, inverse,
    send_sem, recv_sem, meta_send_sem, meta_recv_sem, halo_sem,
):
    me, block = lax.axis_index("blk"), lax.axis_index("shot")
    tiles = owner_ref.shape[1]
    rows = cap * shots
    bf16, f32 = jnp.bfloat16, jnp.float32
    left = lax.rem(block + shot_blocks - 1, shot_blocks)
    right = lax.rem(block + 1, shot_blocks)

    barrier = pltpu.get_barrier_semaphore()

    def greet(i, carry):
        pl.semaphore_signal(
            barrier, inc=1, device_id=(block, lax.rem(me + i, owners)), device_id_type=MESH
        )
        return carry

    lax.fori_loop(1, owners, greet, 0)
    pl.semaphore_signal(barrier, inc=1, device_id=(right, me), device_id_type=MESH)

    relative = lax.rem(owner_ref[...] - me + owners, owners)
    goes = lax.broadcasted_iota(jnp.int32, (owners, tiles), 0) == relative
    goes_bf = goes.astype(f32).astype(bf16)
    before = (
        lax.broadcasted_iota(jnp.int32, (tiles, tiles), 0)
        < lax.broadcasted_iota(jnp.int32, (tiles, tiles), 1)
    ).astype(f32).astype(bf16)
    earlier = dot(goes_bf, before)
    rank = jnp.sum(jnp.where(goes, earlier, 0.0), axis=0, keepdims=True)
    position = relative.astype(f32) * cap + rank

    place = place_ref[...]
    place = lax.rem(place, NSEG) * Q_DEV + lax.div(place, NSEG)
    at_rank = lax.broadcasted_iota(jnp.int32, (FIELD, tiles), 0).astype(f32) == rank
    fields = [
        jnp.where(at_rank, jnp.broadcast_to(f.astype(f32), at_rank.shape), 0.0)
        for f in (place, kind_ref[...], len_ref[...])
    ]
    fields = jnp.concatenate(fields + [jnp.zeros((FIELD, tiles), f32)], axis=0).astype(bf16)
    meta[...] = dot(goes_bf, fields, 1)

    def lay_meta(i, carry):
        meta_send[i] = meta[pl.ds(i, 1), :]
        return carry

    lax.fori_loop(0, owners, lay_meta, 0)
    meta_recv[0] = meta_send[0]

    wide[...] = pix_ref[...].astype(f32)
    lengths = len_ref[...].astype(f32)
    lengths = jnp.concatenate(
        [
            jnp.transpose(jnp.broadcast_to(lengths[:, i : i + TP], (TP, TP)))
            for i in range(0, tiles, TP)
        ],
        axis=0,
    )
    live = lax.broadcasted_iota(jnp.int32, (tiles, TP), 1).astype(f32) < lengths
    masked = jnp.concatenate(
        [
            jnp.where(live, wide[pl.ds(s, tiles, stride=shots), :], 0.0).astype(bf16)
            for s in range(shots)
        ],
        axis=1,
    )

    per = 8

    def pack(c, carry):
        spot = lax.broadcasted_iota(jnp.int32, (per * cap, tiles), 0) + c * (per * cap)
        placing = (spot.astype(f32) == position).astype(f32).astype(bf16)
        packed = dot(placing, masked)
        for d in range(per):
            mine = packed[d * cap : (d + 1) * cap]
            mine = jnp.concatenate([mine[:, s * TP : (s + 1) * TP] for s in range(shots)], axis=0)
            send[c * per + d] = mine.astype(bf16)
        return carry

    lax.fori_loop(0, owners // per, pack, 0)
    recv[0] = send[0]

    pl.semaphore_wait(barrier, owners)

    def meta_copy(i):
        return pltpu.make_async_remote_copy(
            src_ref=meta_send.at[i], dst_ref=meta_recv.at[i],
            send_sem=meta_send_sem, recv_sem=meta_recv_sem,
            device_id=(block, lax.rem(me + i, owners)), device_id_type=MESH,
        )

    def pixel_copy(i, g):
        return pltpu.make_async_remote_copy(
            src_ref=send.at[i], dst_ref=recv.at[i],
            send_sem=send_sem, recv_sem=recv_sem.at[g],
            device_id=(block, lax.rem(me + i, owners)), device_id_type=MESH,
        )

    def start_meta(i, carry):
        meta_copy(i).start()
        return carry

    def start_pixels(i, carry):
        pixel_copy(i, lax.div(i, GROUP)).start()
        return carry

    lax.fori_loop(1, owners, start_meta, 0)
    lax.fori_loop(1, owners, start_pixels, 0)

    others = pl.ds(1, owners - 1)
    all_meta = pltpu.make_async_remote_copy(
        src_ref=meta_send.at[others], dst_ref=meta_recv.at[others],
        send_sem=meta_send_sem, recv_sem=meta_recv_sem,
        device_id=(block, lax.rem(me + 1, owners)), device_id_type=MESH,
    )
    all_meta.wait_recv()

    def columns(i, carry):
        turned = jnp.transpose(jnp.broadcast_to(meta_recv[i], (TP, TP)))
        here = pl.ds(pl.multiple_of(i * cap, 8), cap)
        place_col[here, :] = turned[0:cap]
        kind_col[here, :] = turned[FIELD : FIELD + cap]
        len_col[here, :] = turned[2 * FIELD : 2 * FIELD + cap]
        return carry

    lax.fori_loop(0, owners, columns, 0)

    slots = Q_DEV * NSEG
    slot = lax.broadcasted_iota(jnp.int32, (slots, TP), 0).astype(f32)
    for i in range(owners * cap // TP):
        line = jnp.transpose(place_col[i * TP : (i + 1) * TP, :])
        line = jnp.broadcast_to(line[0:1], (slots, TP))
        chosen[:, i * TP : (i + 1) * TP] = (slot == line).astype(f32).astype(bf16)

    weights = jnp.concatenate([weights_ref[k] for k in range(weights_ref.shape[0])], axis=1)
    kinds = weights_ref.shape[0]

    def pick(kind, product):
        picked = product[:, 0:TP]
        for k in range(1, kinds):
            picked = jnp.where(kind == float(k), product[:, k * TP : (k + 1) * TP], picked)
        return picked

    span = GROUP * cap

    def interpolate(g, carry):
        here = pl.ds(pl.multiple_of(g * span, 16), span)
        kind = kind_col[here, :]

        pixels = recv[pl.ds(g * GROUP, GROUP)].reshape(GROUP * rows, TP)
        product = dot(pixels, weights)
        for s in range(shots):
            mine = jnp.concatenate(
                [
                    product[i * rows + s * cap : i * rows + (s + 1) * cap]
                    for i in range(GROUP)
                ],
                axis=0,
            )
            hi, lo = split(pick(kind, mine))
            values[here, 2 * s * TP : (2 * s + 1) * TP] = hi
            values[here, (2 * s + 1) * TP : (2 * s + 2) * TP] = lo
        return carry

    def interpolate_live(g, carry):
        here = pl.ds(pl.multiple_of(g * span, 16), span)
        kind = kind_col[here, :]
        pixel = lax.broadcasted_iota(jnp.int32, (span, TP), 1).astype(f32)
        alive = (pixel < len_col[here, :]).astype(f32).astype(bf16)
        hi, lo = split(pick(kind, dot(alive, weights)))
        values[here, 2 * shots * TP : (2 * shots + 1) * TP] = hi
        values[here, (2 * shots + 1) * TP : (2 * shots + 2) * TP] = lo
        return carry

    def wait_group(first, count, g):
        these = pl.ds(first, count)
        pltpu.make_async_remote_copy(
            src_ref=send.at[these], dst_ref=recv.at[these],
            send_sem=send_sem, recv_sem=recv_sem.at[g],
            device_id=(block, lax.rem(me + 1, owners)), device_id_type=MESH,
        ).wait_recv()

    lax.fori_loop(0, owners // GROUP, interpolate_live, 0)
    wait_group(1, GROUP - 1, 0)
    interpolate(0, 0)

    def receive(g, carry):
        wait_group(g * GROUP, GROUP, g)
        return interpolate(g, carry)

    lax.fori_loop(1, owners // GROUP, receive, 0)

    def gather(s):
        both = dot(chosen[...], values[:, 2 * s * TP : (2 * s + 2) * TP])
        cycles[s] = both[:, :TP] + both[:, TP:]

    gather(0)
    halo_copy = pltpu.make_async_remote_copy(
        src_ref=cycles.at[0], dst_ref=halo,
        send_sem=halo_sem.at[0], recv_sem=halo_sem.at[1],
        device_id=(left, me), device_id_type=MESH,
    )
    halo_copy.start()
    for s in range(1, shots + 1):
        gather(s)

    def put(here, real, imag):
        for j, part in enumerate((real, imag)):
            hi, lo = split(part)
            high[here, j * TP : (j + 1) * TP] = hi
            low[here, j * TP : (j + 1) * TP] = lo

    def forward(ref, s, carry):
        x = [ref[pl.ds(a * Q_DEV, Q_DEV), :] for a in range(NSEG)]
        total = [None] + [x[a] + x[NSEG - a] for a in range(1, HALF)]
        differ = [None] + [x[a] - x[NSEG - a] for a in range(1, HALF)]
        real = cosine_sums(x[0], x[HALF], total)
        imag = sine_sums(differ)
        for k in range(FREQS):
            here = pl.ds(pl.multiple_of(s * ROWS + k * Q_DEV, 16), Q_DEV)
            cos, sin = turns_ref[0, k : k + 1, :], turns_ref[1, k : k + 1, :]
            if k == 0:
                put(here, real[k], jnp.zeros_like(real[k]))
            elif k == HALF:
                put(here, real[k] * cos, real[k] * sin)
            else:
                put(here, real[k] * cos + imag[k] * sin, real[k] * sin - imag[k] * cos)
        return carry

    def transform(first, count):
        here = pl.ds(first * ROWS, count * ROWS)
        hi, lo = high[here, :], low[here, :]
        return dot(jnp.concatenate([hi, lo, hi], axis=1), dft_ref[...])

    def correlate(s, following, target):
        for k in range(FREQS):
            def at(i):
                return pl.ds(pl.multiple_of(i * ROWS + k * Q_DEV, 16), Q_DEV)
            mine = spectra[at(s), :]
            xr, xi = mine[:, :TP], mine[:, TP:]
            if following is None:
                fr, fi = xr * xr + xi * xi, jnp.zeros_like(xr)
            else:
                differ = mine - spectra[at(following), :]
                dr, di = differ[:, :TP], differ[:, TP:]
                fr, fi = xr * dr + xi * di, xr * di - xi * dr
            put(at(target), fr, fi)

    def back(s):
        parts = []
        for k in range(FREQS):
            here = pl.ds(pl.multiple_of(s * ROWS + k * Q_DEV, 16), Q_DEV)
            re, im = inverse[here, :TP], inverse[here, TP:]
            cos, sin = turns_ref[2, k : k + 1, :], turns_ref[3, k : k + 1, :]
            parts.append((re * cos - im * sin, re * sin + im * cos))
        sums = cosine_sums(parts[0][0], parts[HALF][0], [p[0] for p in parts])
        turned = sine_sums([p[1] for p in parts])
        found = [None] * NSEG
        found[0], found[HALF] = sums[0], sums[HALF]
        for a in range(1, HALF):
            found[a], found[NSEG - a] = sums[a] + turned[a], sums[a] - turned[a]
        return found

    lax.fori_loop(0, shots + 1, lambda s, c: forward(cycles.at[s], s, c), 0)
    spectra[0 : (shots + 1) * ROWS, :] = transform(0, shots + 1)

    def correlate_shot(s, carry):
        correlate(s, s + 1, s)
        return carry

    lax.fori_loop(0, shots - 1, correlate_shot, 0)
    correlate(shots, None, shots - 1)
    inverse[0 : shots * ROWS, :] = transform(0, shots)

    mask = back(shots - 1)
    floor = jnp.maximum(0.01 * mask[0][:, 0:1], 1.0)
    for a in range(NSEG):
        cycles[shots, a * Q_DEV : (a + 1) * Q_DEV, :] = 1.0 / jnp.maximum(mask[a], floor)

    def finish(s, source):
        found = back(source)
        for a in range(NSEG):
            share = cycles[shots, a * Q_DEV : (a + 1) * Q_DEV, :]
            out_ref[s, :, a * TP : (a + 1) * TP] = found[a] * share

    def finish_shot(s, carry):
        finish(s, s)
        return carry

    lax.fori_loop(0, shots - 1, finish_shot, 0)

    halo_copy.wait_recv()
    forward(halo, 0, 0)
    spectra[shots * ROWS : (shots + 1) * ROWS, :] = transform(0, 1)
    correlate(shots - 1, shots, 0)
    inverse[0:ROWS, :] = transform(0, 1)
    finish(shots - 1, 0)

    halo_copy.wait_send()
    all_meta.wait_send()
    pltpu.make_async_remote_copy(
        src_ref=send.at[others], dst_ref=recv.at[others],
        send_sem=send_sem, recv_sem=recv_sem.at[0],
        device_id=(block, lax.rem(me + 1, owners)), device_id_type=MESH,
    ).wait_send()


def per_device(intensities, tile_owner, tile_place, tile_kernel, mask_len, interp_weights):
    owners, shot_blocks = lax.axis_size("blk"), lax.axis_size("shot")
    tiles, shots, _ = intensities.shape
    cap = 3 * tiles // owners
    dft, turns = dft_tables()
    bf16, f32 = jnp.bfloat16, jnp.float32
    slots = Q_DEV * NSEG
    return pl.pallas_call(
        functools.partial(kernel, owners, cap, shots, shot_blocks),
        out_shape=jax.ShapeDtypeStruct((shots, Q_DEV, ANG), f32),
        in_specs=[pl.BlockSpec(memory_space=pltpu.VMEM)] * 8,
        out_specs=pl.BlockSpec(memory_space=pltpu.VMEM),
        scratch_shapes=[
            pltpu.VMEM((tiles * shots, TP), f32),
            pltpu.VMEM((owners, cap * shots, TP), bf16),
            pltpu.VMEM((owners, cap * shots, TP), bf16),
            pltpu.VMEM((owners, TP), f32),
            pltpu.VMEM((owners, 1, TP), f32),
            pltpu.VMEM((owners, 1, TP), f32),
            pltpu.VMEM((owners * cap, TP), f32),
            pltpu.VMEM((owners * cap, TP), f32),
            pltpu.VMEM((owners * cap, TP), f32),
            pltpu.VMEM((slots, owners * cap), bf16),
            pltpu.VMEM((owners * cap, (shots + 1) * 2 * TP), bf16),
            pltpu.VMEM((shots + 1, slots, TP), f32),
            pltpu.VMEM((slots, TP), f32),
            pltpu.VMEM(((shots + 1) * ROWS, 2 * TP), bf16),
            pltpu.VMEM(((shots + 1) * ROWS, 2 * TP), bf16),
            pltpu.VMEM(((shots + 1) * ROWS, 2 * TP), f32),
            pltpu.VMEM((shots * ROWS, 2 * TP), f32),
            pltpu.SemaphoreType.DMA,
            pltpu.SemaphoreType.DMA((owners // GROUP,)),
            pltpu.SemaphoreType.DMA,
            pltpu.SemaphoreType.DMA,
            pltpu.SemaphoreType.DMA((2,)),
        ],
        compiler_params=pltpu.CompilerParams(
            collective_id=0, has_side_effects=True, vmem_limit_bytes=40 * 2**20
        ),
        cost_estimate=pl.CostEstimate(
            flops=3 * 10**9, bytes_accessed=2 * 10**6, transcendentals=0
        ),
    )(
        intensities.reshape(tiles * shots, TP),
        tile_owner.reshape(1, tiles),
        tile_place.reshape(1, tiles),
        tile_kernel.reshape(1, tiles),
        mask_len.reshape(1, tiles),
        interp_weights,
        jnp.asarray(dft),
        jnp.asarray(turns),
    )


def solution(mesh):
    placed = (P("blk", "shot", None), P("blk"), P("blk"), P("blk"), P("blk"), P())
    return jax.shard_map(
        per_device, mesh=mesh, in_specs=placed, out_specs=P("shot", "blk", None), check_vma=False
    )
```

```python
import functools
import math

import jax
import jax.numpy as jnp
import numpy as np
from jax import lax
from jax.experimental import pallas as pl
from jax.experimental.pallas import tpu as pltpu
from jax.sharding import PartitionSpec as P

ANG = 2048
TP = 128
Q_DEV = 16
NSEG = 16
HALF = NSEG // 2
FREQS = HALF + 1
ROWS = FREQS * Q_DEV
FIELD = 32
GROUP = 4
BATCH = 8
FIRST = 32
MESH = pl.DeviceIdType.MESH


def dft_tables():
    b = np.arange(TP)
    angle = 2.0 * math.pi * (np.outer(b, b) % TP) / TP
    cos, sin = np.cos(angle), np.sin(angle)
    table = np.block([[cos, -sin], [sin, cos]]).astype(np.float32)
    high = table.astype(jnp.bfloat16)
    low = (table - high.astype(np.float32)).astype(jnp.bfloat16)
    dft = np.concatenate([high, high, low], axis=0)
    twist = 2.0 * math.pi * (np.outer(np.arange(FREQS), b) % ANG) / ANG
    scale = np.full((FREQS, 1), 2.0 / ANG)
    scale[0] = scale[HALF] = 1.0 / ANG
    turns = np.stack(
        [np.cos(twist), -np.sin(twist), scale * np.cos(twist), -scale * np.sin(twist)]
    ).astype(np.float32)
    return dft, turns


def cosine_sums(first, middle, rest):
    c1, c3, r2 = math.cos(math.pi / 8), math.cos(3 * math.pi / 8), math.sqrt(0.5)
    even, odd = first + middle, first - middle
    g, h = rest[2] + rest[6], r2 * (rest[2] - rest[6])
    base = even + rest[4]
    p = [base + g, odd + h, even - rest[4], odd - h, base - g]
    u1, u3 = rest[1] - rest[7], rest[3] - rest[5]
    t1, t3 = rest[1] + rest[7], rest[3] + rest[5]
    q = [t1 + t3, c1 * u1 + c3 * u3, r2 * (t1 - t3), c3 * u1 - c1 * u3]
    low = [p[k] + q[k] for k in range(4)]
    high = [p[k] - q[k] for k in range(3, -1, -1)]
    return low + [p[4]] + high


def sine_sums(v):
    c1, c3, r2 = math.cos(math.pi / 8), math.cos(3 * math.pi / 8), math.sqrt(0.5)
    e = r2 * (v[2] + v[6])
    w = [None, e + v[4], v[2] - v[6], e - v[4]]
    a, b = v[1] + v[7], v[3] + v[5]
    s, t = v[1] - v[7], v[3] - v[5]
    o = [None, c3 * a + c1 * b, r2 * (s + t), c1 * a - c3 * b]
    low = [o[k] + w[k] for k in range(1, 4)]
    high = [o[k] - w[k] for k in range(3, 0, -1)]
    return [None] + low + [s - t] + high


def split(x):
    high = x.astype(jnp.bfloat16)
    return high, (x - high.astype(jnp.float32)).astype(jnp.bfloat16)


def dot(a, b, rhs_dim=0):
    return lax.dot_general(
        a, b, (((1,), (rhs_dim,)), ((), ())), preferred_element_type=jnp.float32
    )


def send_order(owners):
    def hops(i):
        z, y = i // 8, i // 2 % 4
        return min(z, 4 - z) + min(y, 4 - y)

    return [0] + sorted(range(1, owners), key=lambda i: -hops(i))


def layout_tables(owners, cap, tiles):
    order = np.repeat(np.asarray(send_order(owners), np.int32)[:, None], tiles, axis=1)
    j, lane = np.arange(owners * cap)[:, None], np.arange(TP)[None, :]
    source = (j // cap == np.arange(TP)[None, :owners]).astype(jnp.bfloat16)
    entry = ((lane % FIELD == j % cap) & (lane < 3 * FIELD)).astype(np.float32)
    spread = (np.arange(TP)[:, None] // FIELD == np.arange(3 * TP)[None, :] // TP).astype(jnp.bfloat16)
    return order, source, entry, spread


def kernel(
    owners, cap, shots, shot_blocks, operand_count, *refs
):
    hbm, out_ref, rest = refs[:operand_count], refs[operand_count], refs[operand_count + 1 :]
    local, load_sem, rest = rest[:operand_count], rest[operand_count], rest[operand_count + 1 :]
    (
        owner_ref, place_ref, kind_ref, len_ref, order_ref, pix_ref,
        source_ref, entry_ref, spread_ref, weights_ref, turns_ref, dft_ref,
    ) = local
    (
        wide, send, recv, meta, meta_send, meta_recv, fields_col,
        chosen, values, cycles, shares, high, low, spectra, inverse,
        send_sem, first_sem, rest_sem, meta_send_sem, meta_recv_sem, halo_sem,
    ) = rest
    me, block = lax.axis_index("blk"), lax.axis_index("shot")
    tiles = owner_ref.shape[1]
    rows = cap * shots
    halo, mask = shots, shots + 1
    bf16, f32 = jnp.bfloat16, jnp.float32
    left = lax.rem(block + shot_blocks - 1, shot_blocks)
    right = lax.rem(block + 1, shot_blocks)
    order = send_order(owners)

    loads = [
        pltpu.make_async_copy(source, target, load_sem.at[i])
        for i, (source, target) in enumerate(zip(hbm, local))
    ]
    for load in loads:
        load.start()

    barrier = pltpu.get_barrier_semaphore()

    def greet(i, carry):
        pl.semaphore_signal(
            barrier, inc=1, device_id=(block, lax.bitwise_xor(me, i)), device_id_type=MESH
        )
        return carry

    lax.fori_loop(1, owners, greet, 0)
    pl.semaphore_signal(barrier, inc=1, device_id=(right, me), device_id_type=MESH)

    for load in loads[:5]:
        load.wait()

    goes = order_ref[...] == lax.bitwise_xor(owner_ref[...], me)
    goes_bf = goes.astype(f32).astype(bf16)
    before = (
        lax.broadcasted_iota(jnp.int32, (tiles, tiles), 0)
        < lax.broadcasted_iota(jnp.int32, (tiles, tiles), 1)
    ).astype(f32).astype(bf16)
    number = lax.broadcasted_iota(jnp.int32, (owners, tiles), 0).astype(f32)
    earlier = dot(goes_bf, before)
    rank = jnp.sum(jnp.where(goes, earlier, 0.0), axis=0, keepdims=True)
    position = jnp.sum(jnp.where(goes, earlier + number * cap, 0.0), axis=0, keepdims=True)

    place = place_ref[...]
    place = lax.rem(place, NSEG) * Q_DEV + lax.div(place, NSEG)
    at_rank = lax.broadcasted_iota(jnp.int32, (FIELD, tiles), 0).astype(f32) == rank
    fields = [
        jnp.where(at_rank, jnp.broadcast_to(f.astype(f32), at_rank.shape), 0.0)
        for f in (place, kind_ref[...], len_ref[...])
    ]
    fields = jnp.concatenate(fields + [jnp.zeros((FIELD, tiles), f32)], axis=0).astype(bf16)
    meta[...] = dot(goes_bf, fields, 1)

    def lay_meta(i, carry):
        meta_send[i] = meta[pl.ds(i, 1), :]
        return carry

    lax.fori_loop(0, owners, lay_meta, 0)
    meta_recv[0] = meta_send[0]

    loads[5].wait()
    wide[...] = pix_ref[...].astype(f32)
    lengths = len_ref[...].astype(f32)
    lengths = jnp.concatenate(
        [
            jnp.transpose(jnp.broadcast_to(lengths[:, i : i + TP], (TP, TP)))
            for i in range(0, tiles, TP)
        ],
        axis=0,
    )
    live = lax.broadcasted_iota(jnp.int32, (tiles, TP), 1).astype(f32) < lengths
    masked = jnp.concatenate(
        [
            jnp.where(live, wide[pl.ds(s, tiles, stride=shots), :], 0.0).astype(bf16)
            for s in range(shots)
        ],
        axis=1,
    )

    per = 8

    def pack(c, carry):
        spot = lax.broadcasted_iota(jnp.int32, (per * cap, tiles), 0) + c * (per * cap)
        placing = (spot.astype(f32) == position).astype(f32).astype(bf16)
        packed = dot(placing, masked)
        for d in range(per):
            mine = packed[d * cap : (d + 1) * cap]
            mine = jnp.concatenate([mine[:, s * TP : (s + 1) * TP] for s in range(shots)], axis=0)
            send[c * per + d] = mine.astype(bf16)
        return carry

    lax.fori_loop(0, owners // per, pack, 0)
    recv[0] = send[0]

    pl.semaphore_wait(barrier, owners)

    def meta_copy(here, i):
        return pltpu.make_async_remote_copy(
            src_ref=meta_send.at[here], dst_ref=meta_recv.at[here],
            send_sem=meta_send_sem, recv_sem=meta_recv_sem,
            device_id=(block, lax.bitwise_xor(me, i)), device_id_type=MESH,
        )

    def pixel_copy(here, part, sem, i):
        return pltpu.make_async_remote_copy(
            src_ref=send.at[here, part], dst_ref=recv.at[here, part],
            send_sem=send_sem, recv_sem=sem,
            device_id=(block, lax.bitwise_xor(me, i)), device_id_type=MESH,
        )

    first_rows, rest_rows = pl.ds(0, FIRST), pl.ds(FIRST, rows - FIRST)
    for k in range(1, owners):
        meta_copy(k, order[k]).start()
    for k in range(1, owners):
        pixel_copy(k, first_rows, first_sem, order[k]).start()
    for k in range(1, owners):
        pixel_copy(k, rest_rows, rest_sem.at[k // GROUP], order[k]).start()

    others = pl.ds(1, owners - 1)
    for load in loads[6:10]:
        load.wait()
    meta_copy(others, 1).wait_recv()

    entries = dot(source_ref[...], meta_recv[...].reshape(owners, TP).astype(bf16))
    fields_col[...] = dot((entries * entry_ref[...]).astype(bf16), spread_ref[...])
    slots = Q_DEV * NSEG
    slot = lax.broadcasted_iota(jnp.int32, (slots, TP), 0).astype(f32)
    for i in range(owners * cap // TP):
        line = jnp.transpose(fields_col[i * TP : (i + 1) * TP, :TP])
        line = jnp.broadcast_to(line[0:1], (slots, TP))
        chosen[:, i * TP : (i + 1) * TP] = (slot == line).astype(f32).astype(bf16)

    weights = jnp.concatenate([weights_ref[k] for k in range(weights_ref.shape[0])], axis=1)
    kinds = weights_ref.shape[0]

    def pick(kind, product):
        picked = product[:, 0:TP]
        for k in range(1, kinds):
            picked = jnp.where(kind == float(k), product[:, k * TP : (k + 1) * TP], picked)
        return picked

    def keep(here, column, kind, product):
        hi, lo = split(pick(kind, product))
        values[here, 2 * column * TP : (2 * column + 1) * TP] = hi
        values[here, (2 * column + 1) * TP : (2 * column + 2) * TP] = lo

    def interpolate(g, count, start, end, first_shot, last_shot):
        here = pl.ds(pl.multiple_of(g * (count * cap), 16), count * cap)
        kind = fields_col[here, TP : 2 * TP]
        size = end - start
        pixels = recv[pl.ds(g * count, count), start:end].reshape(count * size, TP)
        product = dot(pixels, weights)
        for s in range(first_shot, last_shot):
            mine = [
                product[i * size + s * cap - start : i * size + (s + 1) * cap - start]
                for i in range(count)
            ]
            keep(here, s, kind, jnp.concatenate(mine, axis=0))

    def interpolate_live(g, carry):
        span = BATCH * cap
        here = pl.ds(pl.multiple_of(g * span, 16), span)
        pixel = lax.broadcasted_iota(jnp.int32, (span, TP), 1).astype(f32)
        alive = (pixel < fields_col[here, 2 * TP :]).astype(f32).astype(bf16)
        keep(here, shots, fields_col[here, TP : 2 * TP], dot(alive, weights))
        return carry

    lax.fori_loop(0, owners // BATCH, interpolate_live, 0)

    def gather(s, target):
        both = dot(chosen[...], values[:, 2 * s * TP : (2 * s + 2) * TP])
        cycles[target] = both[:, :TP] + both[:, TP:]

    gather(shots, mask)

    def interpolate_first(g, carry):
        interpolate(g, BATCH, 0, FIRST, 0, 1)
        return carry

    pixel_copy(others, first_rows, first_sem, 1).wait_recv()
    lax.fori_loop(0, owners // BATCH, interpolate_first, 0)
    gather(0, 0)
    halo_copy = pltpu.make_async_remote_copy(
        src_ref=cycles.at[0], dst_ref=cycles.at[halo],
        send_sem=halo_sem.at[0], recv_sem=halo_sem.at[1],
        device_id=(left, me), device_id_type=MESH,
    )
    halo_copy.start()

    def put(here, real, imag):
        for j, part in enumerate((real, imag)):
            hi, lo = split(part)
            high[here, j * TP : (j + 1) * TP] = hi
            low[here, j * TP : (j + 1) * TP] = lo

    def band(s, k):
        return pl.ds(pl.multiple_of(s * ROWS + k * Q_DEV, 16), Q_DEV)

    def forward(s, target):
        x = [cycles[s, a * Q_DEV : (a + 1) * Q_DEV, :] for a in range(NSEG)]
        total = [None] + [x[a] + x[NSEG - a] for a in range(1, HALF)]
        differ = [None] + [x[a] - x[NSEG - a] for a in range(1, HALF)]
        real = cosine_sums(x[0], x[HALF], total)
        imag = sine_sums(differ)
        for k in range(FREQS):
            here = band(target, k)
            cos, sin = turns_ref[0, k : k + 1, :], turns_ref[1, k : k + 1, :]
            if k == 0:
                put(here, real[k], jnp.zeros_like(real[k]))
            elif k == HALF:
                put(here, real[k] * cos, real[k] * sin)
            else:
                put(here, real[k] * cos + imag[k] * sin, real[k] * sin - imag[k] * cos)

    def transform(first, count):
        here = pl.ds(first * ROWS, count * ROWS)
        hi, lo = high[here, :], low[here, :]
        return dot(jnp.concatenate([hi, lo, hi], axis=1), dft_ref[...])

    def correlate(s, following, target):
        for k in range(FREQS):
            mine = spectra[band(s, k), :]
            xr, xi = mine[:, :TP], mine[:, TP:]
            if following is None:
                put(band(target, k), xr * xr + xi * xi, jnp.zeros_like(xr))
            else:
                differ = mine - spectra[band(following, k), :]
                dr, di = differ[:, :TP], differ[:, TP:]
                put(band(target, k), xr * dr + xi * di, xr * di - xi * dr)

    def back(s):
        parts = []
        for k in range(FREQS):
            here = band(s, k)
            re, im = inverse[here, :TP], inverse[here, TP:]
            cos, sin = turns_ref[2, k : k + 1, :], turns_ref[3, k : k + 1, :]
            parts.append((re * cos - im * sin, re * sin + im * cos))
        sums = cosine_sums(parts[0][0], parts[HALF][0], [p[0] for p in parts])
        turned = sine_sums([p[1] for p in parts])
        found = [None] * NSEG
        found[0], found[HALF] = sums[0], sums[HALF]
        for a in range(1, HALF):
            found[a], found[NSEG - a] = sums[a] + turned[a], sums[a] - turned[a]
        return found

    for load in loads[10:]:
        load.wait()
    forward(0, 0)
    forward(mask, 1)
    spectra[0 : 2 * ROWS, :] = transform(0, 2)
    correlate(1, None, 0)
    inverse[0:ROWS, :] = transform(0, 1)
    overlap = back(0)
    floor = jnp.maximum(0.01 * overlap[0][:, 0:1], 1.0)
    for a in range(NSEG):
        shares[a * Q_DEV : (a + 1) * Q_DEV, :] = 1.0 / jnp.maximum(overlap[a], floor)

    def receive(first, count, g):
        pixel_copy(pl.ds(first, count), rest_rows, rest_sem.at[g], 1).wait_recv()

    receive(1, GROUP - 1, 0)
    interpolate(0, GROUP, 16, rows, 1, shots)

    def take_group(g, carry):
        receive(g * GROUP, GROUP, g)
        interpolate(g, GROUP, 16, rows, 1, shots)
        return carry

    lax.fori_loop(1, owners // GROUP, take_group, 0)
    for s in range(1, shots):
        gather(s, s)
    halo_copy.wait_recv()

    def forward_shot(s, carry):
        forward(s, s)
        return carry

    lax.fori_loop(1, shots + 1, forward_shot, 0)
    spectra[ROWS : (shots + 1) * ROWS, :] = transform(1, shots)

    def correlate_shot(s, carry):
        correlate(s, s + 1, s)
        return carry

    lax.fori_loop(0, shots, correlate_shot, 0)
    inverse[0 : shots * ROWS, :] = transform(0, shots)

    def finish_shot(s, carry):
        found = back(s)
        for a in range(NSEG):
            share = shares[a * Q_DEV : (a + 1) * Q_DEV, :]
            out_ref[s, :, a * TP : (a + 1) * TP] = found[a] * share
        return carry

    lax.fori_loop(0, shots, finish_shot, 0)

    halo_copy.wait_send()
    meta_copy(others, 1).wait_send()
    pixel_copy(others, pl.ds(0, rows), first_sem, 1).wait_send()


def per_device(intensities, tile_owner, tile_place, tile_kernel, mask_len, interp_weights):
    owners, shot_blocks = lax.axis_size("blk"), lax.axis_size("shot")
    tiles, shots, _ = intensities.shape
    cap = 3 * tiles // owners
    dft, turns = dft_tables()
    order, source, entry, spread = layout_tables(owners, cap, tiles)
    bf16, f32 = jnp.bfloat16, jnp.float32
    slots = Q_DEV * NSEG
    operands = (
        tile_owner.reshape(1, tiles),
        tile_place.reshape(1, tiles),
        tile_kernel.reshape(1, tiles),
        mask_len.reshape(1, tiles),
        jnp.asarray(order),
        intensities.reshape(tiles * shots, TP),
        jnp.asarray(source),
        jnp.asarray(entry),
        jnp.asarray(spread),
        interp_weights,
        jnp.asarray(turns),
        jnp.asarray(dft),
    )
    return pl.pallas_call(
        functools.partial(kernel, owners, cap, shots, shot_blocks, len(operands)),
        out_shape=jax.ShapeDtypeStruct((shots, Q_DEV, ANG), f32),
        in_specs=[pl.BlockSpec(memory_space=pltpu.HBM)] * len(operands),
        out_specs=pl.BlockSpec(memory_space=pltpu.VMEM),
        scratch_shapes=[pltpu.VMEM(x.shape, x.dtype) for x in operands]
        + [pltpu.SemaphoreType.DMA((len(operands),))]
        + [
            pltpu.VMEM((tiles * shots, TP), f32),
            pltpu.VMEM((owners, cap * shots, TP), bf16),
            pltpu.VMEM((owners, cap * shots, TP), bf16),
            pltpu.VMEM((owners, TP), f32),
            pltpu.VMEM((owners, 1, TP), f32),
            pltpu.VMEM((owners, 1, TP), f32),
            pltpu.VMEM((owners * cap, 3 * TP), f32),
            pltpu.VMEM((slots, owners * cap), bf16),
            pltpu.VMEM((owners * cap, (shots + 1) * 2 * TP), bf16),
            pltpu.VMEM((shots + 2, slots, TP), f32),
            pltpu.VMEM((slots, TP), f32),
            pltpu.VMEM(((shots + 1) * ROWS, 2 * TP), bf16),
            pltpu.VMEM(((shots + 1) * ROWS, 2 * TP), bf16),
            pltpu.VMEM(((shots + 1) * ROWS, 2 * TP), f32),
            pltpu.VMEM((shots * ROWS, 2 * TP), f32),
            pltpu.SemaphoreType.DMA,
            pltpu.SemaphoreType.DMA,
            pltpu.SemaphoreType.DMA((owners // GROUP,)),
            pltpu.SemaphoreType.DMA,
            pltpu.SemaphoreType.DMA,
            pltpu.SemaphoreType.DMA((2,)),
        ],
        compiler_params=pltpu.CompilerParams(
            collective_id=0, has_side_effects=True, vmem_limit_bytes=40 * 2**20
        ),
        cost_estimate=pl.CostEstimate(
            flops=3 * 10**9, bytes_accessed=2 * 10**6, transcendentals=0
        ),
    )(*(pltpu.with_memory_space_constraint(x, pltpu.HBM) for x in operands))


def solution(mesh):
    placed = (P("blk", "shot", None), P("blk"), P("blk"), P("blk"), P("blk"), P())
    return jax.shard_map(
        per_device, mesh=mesh, in_specs=placed, out_specs=P("shot", "blk", None), check_vma=False
    )
```

```python
import functools
import math

import jax
import jax.numpy as jnp
import numpy as np
from jax import lax
from jax.experimental import pallas as pl
from jax.experimental.pallas import tpu as pltpu
from jax.sharding import PartitionSpec as P

ANG = 2048
TP = 128
Q_DEV = 16
NSEG = 16
HALF = NSEG // 2
FREQS = HALF + 1
ROWS = FREQS * Q_DEV
FIELD = 32
STARTS = (0, 16, 32)
BATCH = 16
LATE = 1
MESH = pl.DeviceIdType.MESH


def dft_tables():
    b = np.arange(TP)
    angle = 2.0 * math.pi * (np.outer(b, b) % TP) / TP
    cos, sin = np.cos(angle), np.sin(angle)
    table = np.block([[cos, -sin], [sin, cos]]).astype(np.float32)
    high = table.astype(jnp.bfloat16)
    low = (table - high.astype(np.float32)).astype(jnp.bfloat16)
    dft = np.concatenate([high, high, low], axis=0)
    twist = 2.0 * math.pi * (np.outer(np.arange(FREQS), b) % ANG) / ANG
    scale = np.full((FREQS, 1), 2.0 / ANG)
    scale[0] = scale[HALF] = 1.0 / ANG
    turns = np.stack(
        [np.cos(twist), -np.sin(twist), scale * np.cos(twist), -scale * np.sin(twist)]
    ).astype(np.float32)
    return dft, turns


def cosine_sums(first, middle, rest):
    c1, c3, r2 = math.cos(math.pi / 8), math.cos(3 * math.pi / 8), math.sqrt(0.5)
    even, odd = first + middle, first - middle
    g, h = rest[2] + rest[6], r2 * (rest[2] - rest[6])
    base = even + rest[4]
    p = [base + g, odd + h, even - rest[4], odd - h, base - g]
    u1, u3 = rest[1] - rest[7], rest[3] - rest[5]
    t1, t3 = rest[1] + rest[7], rest[3] + rest[5]
    q = [t1 + t3, c1 * u1 + c3 * u3, r2 * (t1 - t3), c3 * u1 - c1 * u3]
    low = [p[k] + q[k] for k in range(4)]
    high = [p[k] - q[k] for k in range(3, -1, -1)]
    return low + [p[4]] + high


def sine_sums(v):
    c1, c3, r2 = math.cos(math.pi / 8), math.cos(3 * math.pi / 8), math.sqrt(0.5)
    e = r2 * (v[2] + v[6])
    w = [None, e + v[4], v[2] - v[6], e - v[4]]
    a, b = v[1] + v[7], v[3] + v[5]
    s, t = v[1] - v[7], v[3] - v[5]
    o = [None, c3 * a + c1 * b, r2 * (s + t), c1 * a - c3 * b]
    low = [o[k] + w[k] for k in range(1, 4)]
    high = [o[k] - w[k] for k in range(3, 0, -1)]
    return [None] + low + [s - t] + high


def split(x):
    high = x.astype(jnp.bfloat16)
    return high, (x - high.astype(jnp.float32)).astype(jnp.bfloat16)


def dot(a, b, rhs_dim=0):
    return lax.dot_general(
        a, b, (((1,), (rhs_dim,)), ((), ())), preferred_element_type=jnp.float32
    )


def send_order(owners):
    def hops(i):
        z, y = i // 8, i // 2 % 4
        return min(z, 4 - z) + min(y, 4 - y)

    return [0] + sorted(range(1, owners), key=lambda i: -hops(i))


def layout_tables(owners, cap, tiles):
    order = np.repeat(np.asarray(send_order(owners), np.int32)[:, None], tiles, axis=1)
    j, lane = np.arange(owners * cap)[:, None], np.arange(TP)[None, :]
    source = (j // cap == np.arange(TP)[None, :owners]).astype(jnp.bfloat16)
    entry = ((lane % FIELD == j % cap) & (lane < 3 * FIELD)).astype(np.float32)
    spread = (np.arange(TP)[:, None] // FIELD == np.arange(3 * TP)[None, :] // TP).astype(jnp.bfloat16)
    return order, source, entry, spread


def kernel(
    owners, cap, shots, shot_blocks, operand_count, *refs
):
    hbm, out_ref, rest = refs[:operand_count], refs[operand_count], refs[operand_count + 1 :]
    local, load_sem, rest = rest[:operand_count], rest[operand_count], rest[operand_count + 1 :]
    (
        owner_ref, place_ref, kind_ref, len_ref, order_ref, pix_ref,
        source_ref, entry_ref, spread_ref, weights_ref, turns_ref, dft_ref,
    ) = local
    (
        wide, send, recv, meta, meta_send, meta_recv, fields_col,
        is_kind, chosen, values, cycles, shares, high, low, spectra, inverse,
        send_sem, piece_sem, meta_send_sem, meta_recv_sem, halo_sem,
    ) = rest
    me, block = lax.axis_index("blk"), lax.axis_index("shot")
    tiles = owner_ref.shape[1]
    rows = cap * shots
    halo, mask = shots, shots + 1
    turned_back = shots + 2
    bf16, f32 = jnp.bfloat16, jnp.float32
    left = lax.rem(block + shot_blocks - 1, shot_blocks)
    right = lax.rem(block + 1, shot_blocks)
    order = send_order(owners)

    barrier = pltpu.get_barrier_semaphore()
    pl.semaphore_signal(barrier, inc=1, device_id=(right, me), device_id_type=MESH)
    for k in range(1, owners):
        pl.semaphore_signal(
            barrier,
            inc=1,
            device_id=(block, lax.bitwise_xor(me, order[k])),
            device_id_type=MESH,
        )

    loads = [
        pltpu.make_async_copy(source, target, load_sem.at[i])
        for i, (source, target) in enumerate(zip(hbm, local))
    ]
    for load in loads:
        load.start()

    for load in loads[:5]:
        load.wait()

    goes = order_ref[...] == lax.bitwise_xor(owner_ref[...], me)
    goes_bf = goes.astype(f32).astype(bf16)
    before = (
        lax.broadcasted_iota(jnp.int32, (tiles, tiles), 0)
        < lax.broadcasted_iota(jnp.int32, (tiles, tiles), 1)
    ).astype(f32).astype(bf16)
    number = lax.broadcasted_iota(jnp.int32, (owners, tiles), 0).astype(f32)
    earlier = dot(goes_bf, before)
    rank = jnp.sum(jnp.where(goes, earlier, 0.0), axis=0, keepdims=True)
    position = jnp.sum(jnp.where(goes, earlier + number * cap, 0.0), axis=0, keepdims=True)

    place = place_ref[...]
    place = lax.rem(place, NSEG) * Q_DEV + lax.div(place, NSEG)
    at_rank = lax.broadcasted_iota(jnp.int32, (FIELD, tiles), 0).astype(f32) == rank
    fields = [
        jnp.where(at_rank, jnp.broadcast_to(f.astype(f32), at_rank.shape), 0.0)
        for f in (place, kind_ref[...], len_ref[...])
    ]
    fields = jnp.concatenate(fields + [jnp.zeros((FIELD, tiles), f32)], axis=0).astype(bf16)
    meta[...] = dot(goes_bf, fields, 1)

    def lay_meta(i, carry):
        meta_send[i] = meta[pl.ds(i, 1), :]
        return carry

    lax.fori_loop(0, owners, lay_meta, 0)
    meta_recv[0] = meta_send[0]

    loads[5].wait()
    wide[...] = pix_ref[...].astype(f32)
    lengths = len_ref[...].astype(f32)
    lengths = jnp.concatenate(
        [
            jnp.transpose(jnp.broadcast_to(lengths[:, i : i + TP], (TP, TP)))
            for i in range(0, tiles, TP)
        ],
        axis=0,
    )
    live = lax.broadcasted_iota(jnp.int32, (tiles, TP), 1).astype(f32) < lengths
    masked = jnp.concatenate(
        [
            jnp.where(live, wide[pl.ds(s, tiles, stride=shots), :], 0.0).astype(bf16)
            for s in range(shots)
        ],
        axis=1,
    )

    def meta_copy(here, i):
        return pltpu.make_async_remote_copy(
            src_ref=meta_send.at[here], dst_ref=meta_recv.at[here],
            send_sem=meta_send_sem, recv_sem=meta_recv_sem,
            device_id=(block, lax.bitwise_xor(me, i)), device_id_type=MESH,
        )

    def pixel_copy(here, part, sem, i):
        return pltpu.make_async_remote_copy(
            src_ref=send.at[here, part], dst_ref=recv.at[here, part],
            send_sem=send_sem, recv_sem=sem,
            device_id=(block, lax.bitwise_xor(me, i)), device_id_type=MESH,
        )

    def group_of(k):
        return sum(k >= start for start in STARTS[1:-1])

    third = rows // 3
    pieces = [pl.ds(part * third, third) for part in range(3)]

    def pack(first, count):
        spot = lax.broadcasted_iota(jnp.int32, (count * cap, tiles), 0) + first * cap
        placing = (spot.astype(f32) == position).astype(f32).astype(bf16)
        packed = dot(placing, masked)
        for d in range(count):
            mine = packed[d * cap : (d + 1) * cap]
            mine = jnp.concatenate([mine[:, s * TP : (s + 1) * TP] for s in range(shots)], axis=0)
            send[first + d] = mine.astype(bf16)

    for first in range(0, owners, BATCH):
        pack(first, BATCH)
    recv[0] = send[0]

    pl.semaphore_wait(barrier, owners)
    for k in range(1, owners):
        meta_copy(k, order[k]).start()
    for part in range(2):
        for k in range(1, owners):
            pixel_copy(k, pieces[part], piece_sem.at[part], order[k]).start()
    for k in range(1, owners):
        pixel_copy(k, pieces[2], piece_sem.at[2 + group_of(k)], order[k]).start()

    others = pl.ds(1, owners - 1)
    for load in loads[6:10]:
        load.wait()
    meta_copy(others, 1).wait_recv()

    entries = dot(source_ref[...], meta_recv[...].reshape(owners, TP).astype(bf16))
    fields_col[...] = dot((entries * entry_ref[...]).astype(bf16), spread_ref[...])
    slots = Q_DEV * NSEG
    slot = lax.broadcasted_iota(jnp.int32, (slots, TP), 0).astype(f32)
    for i in range(owners * cap // TP):
        line = jnp.transpose(fields_col[i * TP : (i + 1) * TP, :TP])
        line = jnp.broadcast_to(line[0:1], (slots, TP))
        chosen[:, i * TP : (i + 1) * TP] = (slot == line).astype(f32).astype(bf16)

    kinds = weights_ref.shape[0]
    weights = weights_ref[...].reshape(kinds * TP, TP)

    def mark_kinds(i, carry):
        kind = fields_col[pl.ds(pl.multiple_of(i * cap, 8), cap), TP : 2 * TP]
        for k in range(kinds):
            one = (kind == float(k)).astype(f32)
            is_kind[k, i] = jnp.concatenate([one] * shots, axis=0).astype(bf16)
        return carry

    def keep(here, column, product):
        hi, lo = split(product)
        values[here, 2 * column * TP : (2 * column + 1) * TP] = hi
        values[here, (2 * column + 1) * TP : (2 * column + 2) * TP] = lo

    def interpolate(first, count, start, end, first_shot, last_shot):
        here = pl.ds(pl.multiple_of(first * cap, 16), count * cap)
        size, these = end - start, pl.ds(first, count)
        pixels = recv[these, start:end].reshape(count * size, TP)
        spread = [
            pixels * is_kind[k, these, start:end].reshape(count * size, TP) for k in range(kinds)
        ]
        product = dot(jnp.concatenate(spread, axis=1), weights)
        for s in range(first_shot, last_shot):
            mine = [
                product[i * size + s * cap - start : i * size + (s + 1) * cap - start]
                for i in range(count)
            ]
            keep(here, s, jnp.concatenate(mine, axis=0))

    def interpolate_live(g, carry):
        span = BATCH * cap
        here = pl.ds(pl.multiple_of(g * span, 16), span)
        pixel = lax.broadcasted_iota(jnp.int32, (span, TP), 1).astype(f32)
        kind = fields_col[here, TP : 2 * TP]
        alive = jnp.where(pixel < fields_col[here, 2 * TP :], kind, -1.0)
        spread = [(alive == float(k)).astype(f32).astype(bf16) for k in range(kinds)]
        keep(here, shots, dot(jnp.concatenate(spread, axis=1), weights))
        return carry

    lax.fori_loop(0, owners // BATCH, interpolate_live, 0)
    lax.fori_loop(0, owners, mark_kinds, 0)

    def gather(s, target, start=0, end=owners * cap):
        both = dot(chosen[:, start:end], values[start:end, 2 * s * TP : (2 * s + 2) * TP])
        both = both[:, :TP] + both[:, TP:]
        cycles[target] = both + cycles[target] if start else both

    gather(shots, mask)

    def put(here, real, imag):
        for j, part in enumerate((real, imag)):
            hi, lo = split(part)
            high[here, j * TP : (j + 1) * TP] = hi
            low[here, j * TP : (j + 1) * TP] = lo

    def band(s, k):
        return pl.ds(pl.multiple_of(s * ROWS + k * Q_DEV, 16), Q_DEV)

    def forward(s):
        x = [cycles[s, a * Q_DEV : (a + 1) * Q_DEV, :] for a in range(NSEG)]
        total = [None] + [x[a] + x[NSEG - a] for a in range(1, HALF)]
        differ = [None] + [x[a] - x[NSEG - a] for a in range(1, HALF)]
        real = cosine_sums(x[0], x[HALF], total)
        imag = sine_sums(differ)
        for k in range(FREQS):
            here = band(s, k)
            cos, sin = turns_ref[0, k : k + 1, :], turns_ref[1, k : k + 1, :]
            if k == 0:
                put(here, real[k], jnp.zeros_like(real[k]))
            elif k == HALF:
                put(here, real[k] * cos, real[k] * sin)
            else:
                put(here, real[k] * cos + imag[k] * sin, real[k] * sin - imag[k] * cos)

    def transform(result, target, first, count):
        here = pl.ds(first * ROWS, count * ROWS)
        hi, lo = high[here, :], low[here, :]
        found = dot(jnp.concatenate([hi, lo, hi], axis=1), dft_ref[...])
        result[pl.ds(target * ROWS, count * ROWS), :] = found

    def correlate(s, following, target):
        for k in range(FREQS):
            mine = spectra[band(s, k), :]
            xr, xi = mine[:, :TP], mine[:, TP:]
            if following is None:
                put(band(target, k), xr * xr + xi * xi, jnp.zeros_like(xr))
            else:
                differ = mine - spectra[band(following, k), :]
                dr, di = differ[:, :TP], differ[:, TP:]
                put(band(target, k), xr * dr + xi * di, xr * di - xi * dr)

    def back(s):
        parts = []
        for k in range(FREQS):
            here = band(s, k)
            re, im = inverse[here, :TP], inverse[here, TP:]
            cos, sin = turns_ref[2, k : k + 1, :], turns_ref[3, k : k + 1, :]
            parts.append((re * cos - im * sin, re * sin + im * cos))
        sums = cosine_sums(parts[0][0], parts[HALF][0], [p[0] for p in parts])
        turned = sine_sums([p[1] for p in parts])
        found = [None] * NSEG
        found[0], found[HALF] = sums[0], sums[HALF]
        for a in range(1, HALF):
            found[a], found[NSEG - a] = sums[a] + turned[a], sums[a] - turned[a]
        return found

    for load in loads[10:]:
        load.wait()
    forward(mask)
    transform(spectra, mask, mask, 1)
    correlate(mask, None, turned_back + shots)
    transform(inverse, shots, turned_back + shots, 1)
    overlap = back(shots)
    floor = jnp.maximum(0.01 * overlap[0][:, 0:1], 1.0)
    for a in range(NSEG):
        shares[a * Q_DEV : (a + 1) * Q_DEV, :] = 1.0 / jnp.maximum(overlap[a], floor)

    def finish(s):
        found = back(s)
        for a in range(NSEG):
            share = shares[a * Q_DEV : (a + 1) * Q_DEV, :]
            out_ref[s, :, a * TP : (a + 1) * TP] = found[a] * share

    pixel_copy(others, pieces[0], piece_sem.at[0], 1).wait_recv()
    for first in range(0, owners, BATCH):
        interpolate(first, BATCH, 0, third, 0, 1)
    gather(0, 0)
    halo_copy = pltpu.make_async_remote_copy(
        src_ref=cycles.at[0], dst_ref=cycles.at[halo],
        send_sem=halo_sem.at[0], recv_sem=halo_sem.at[1],
        device_id=(left, me), device_id_type=MESH,
    )
    halo_copy.start()
    forward(0)
    transform(spectra, 0, 0, 1)

    pixel_copy(others, pieces[1], piece_sem.at[1], 1).wait_recv()
    for first in range(0, owners, BATCH):
        interpolate(first, BATCH, 16, 48, 1, 2)
    gather(1, 1)
    forward(1)
    transform(spectra, 1, 1, 1)
    correlate(0, 1, turned_back)
    transform(inverse, 0, turned_back, 1)
    finish(0)

    def take_group(g):
        skip = 1 if g == 0 else 0
        pixel_copy(
            pl.ds(STARTS[g] + skip, STARTS[g + 1] - STARTS[g] - skip),
            pieces[2],
            piece_sem.at[2 + g],
            1,
        ).wait_recv()
        interpolate(STARTS[g], STARTS[g + 1] - STARTS[g], 48, rows, 2, shots)

    groups = len(STARTS) - 1
    early = STARTS[groups - LATE] * cap
    for g in range(groups - LATE):
        take_group(g)
    for s in range(2, shots):
        gather(s, s, 0, early)
    for g in range(groups - LATE, groups):
        take_group(g)
    for s in range(2, shots):
        gather(s, s, early, owners * cap)
        forward(s)
    halo_copy.wait_recv()
    forward(halo)
    transform(spectra, 2, 2, shots - 1)
    for s in range(1, shots):
        correlate(s, s + 1, turned_back + s)
    transform(inverse, 1, turned_back + 1, shots - 1)
    for s in range(1, shots):
        finish(s)

    halo_copy.wait_send()
    meta_copy(others, 1).wait_send()
    pixel_copy(others, pl.ds(0, rows), piece_sem.at[0], 1).wait_send()


def per_device(intensities, tile_owner, tile_place, tile_kernel, mask_len, interp_weights):
    owners, shot_blocks = lax.axis_size("blk"), lax.axis_size("shot")
    tiles, shots, _ = intensities.shape
    cap = 3 * tiles // owners
    dft, turns = dft_tables()
    order, source, entry, spread = layout_tables(owners, cap, tiles)
    bf16, f32 = jnp.bfloat16, jnp.float32
    slots = Q_DEV * NSEG
    operands = (
        tile_owner.reshape(1, tiles),
        tile_place.reshape(1, tiles),
        tile_kernel.reshape(1, tiles),
        mask_len.reshape(1, tiles),
        jnp.asarray(order),
        intensities.reshape(tiles * shots, TP),
        jnp.asarray(source),
        jnp.asarray(entry),
        jnp.asarray(spread),
        interp_weights,
        jnp.asarray(turns),
        jnp.asarray(dft),
    )
    return pl.pallas_call(
        functools.partial(kernel, owners, cap, shots, shot_blocks, len(operands)),
        out_shape=jax.ShapeDtypeStruct((shots, Q_DEV, ANG), f32),
        in_specs=[pl.BlockSpec(memory_space=pltpu.HBM)] * len(operands),
        out_specs=pl.BlockSpec(memory_space=pltpu.VMEM),
        scratch_shapes=[pltpu.VMEM(x.shape, x.dtype) for x in operands]
        + [pltpu.SemaphoreType.DMA((len(operands),))]
        + [
            pltpu.VMEM((tiles * shots, TP), f32),
            pltpu.VMEM((owners, cap * shots, TP), bf16),
            pltpu.VMEM((owners, cap * shots, TP), bf16),
            pltpu.VMEM((owners, TP), f32),
            pltpu.VMEM((owners, 1, TP), f32),
            pltpu.VMEM((owners, 1, TP), f32),
            pltpu.VMEM((owners * cap, 3 * TP), f32),
            pltpu.VMEM((interp_weights.shape[0], owners, cap * shots, TP), bf16),
            pltpu.VMEM((slots, owners * cap), bf16),
            pltpu.VMEM((owners * cap, (shots + 1) * 2 * TP), bf16),
            pltpu.VMEM((shots + 2, slots, TP), f32),
            pltpu.VMEM((slots, TP), f32),
            pltpu.VMEM(((2 * shots + 3) * ROWS, 2 * TP), bf16),
            pltpu.VMEM(((2 * shots + 3) * ROWS, 2 * TP), bf16),
            pltpu.VMEM(((shots + 2) * ROWS, 2 * TP), f32),
            pltpu.VMEM(((shots + 1) * ROWS, 2 * TP), f32),
            pltpu.SemaphoreType.DMA,
            pltpu.SemaphoreType.DMA((len(STARTS) + 1,)),
            pltpu.SemaphoreType.DMA,
            pltpu.SemaphoreType.DMA,
            pltpu.SemaphoreType.DMA((2,)),
        ],
        compiler_params=pltpu.CompilerParams(
            collective_id=0, has_side_effects=True, vmem_limit_bytes=40 * 2**20
        ),
        cost_estimate=pl.CostEstimate(
            flops=3 * 10**9, bytes_accessed=2 * 10**6, transcendentals=0
        ),
    )(*(pltpu.with_memory_space_constraint(x, pltpu.HBM) for x in operands))


def solution(mesh):
    placed = (P("blk", "shot", None), P("blk"), P("blk"), P("blk"), P("blk"), P())
    return jax.shard_map(
        per_device, mesh=mesh, in_specs=placed, out_specs=P("shot", "blk", None), check_vma=False
    )
```

```python
import functools
import math

import jax
import jax.numpy as jnp
import numpy as np
from jax import lax
from jax.experimental import pallas as pl
from jax.experimental.pallas import tpu as pltpu
from jax.sharding import PartitionSpec as P

ANG = 2048
TP = 128
Q_DEV = 16
NSEG = 16
HALF = NSEG // 2
FREQS = HALF + 1
ROWS = FREQS * Q_DEV
FIELD = 32
STARTS = (0, 16, 32)
BATCH = 16
LATE = 1
MESH = pl.DeviceIdType.MESH


def dft_tables():
    b = np.arange(TP)
    angle = 2.0 * math.pi * (np.outer(b, b) % TP) / TP
    cos, sin = np.cos(angle), np.sin(angle)
    table = np.block([[cos, -sin], [sin, cos]]).astype(np.float32)
    high = table.astype(jnp.bfloat16)
    low = (table - high.astype(np.float32)).astype(jnp.bfloat16)
    dft = np.concatenate([high, high, low], axis=0)
    twist = 2.0 * math.pi * (np.outer(np.arange(FREQS), b) % ANG) / ANG
    scale = np.full((FREQS, 1), 2.0 / ANG)
    scale[0] = scale[HALF] = 1.0 / ANG
    turns = np.stack(
        [np.cos(twist), -np.sin(twist), scale * np.cos(twist), -scale * np.sin(twist)]
    ).astype(np.float32)
    return dft, turns


def cosine_sums(first, middle, rest):
    c1, c3, r2 = math.cos(math.pi / 8), math.cos(3 * math.pi / 8), math.sqrt(0.5)
    even, odd = first + middle, first - middle
    g, h = rest[2] + rest[6], r2 * (rest[2] - rest[6])
    base = even + rest[4]
    p = [base + g, odd + h, even - rest[4], odd - h, base - g]
    u1, u3 = rest[1] - rest[7], rest[3] - rest[5]
    t1, t3 = rest[1] + rest[7], rest[3] + rest[5]
    q = [t1 + t3, c1 * u1 + c3 * u3, r2 * (t1 - t3), c3 * u1 - c1 * u3]
    low = [p[k] + q[k] for k in range(4)]
    high = [p[k] - q[k] for k in range(3, -1, -1)]
    return low + [p[4]] + high


def sine_sums(v):
    c1, c3, r2 = math.cos(math.pi / 8), math.cos(3 * math.pi / 8), math.sqrt(0.5)
    e = r2 * (v[2] + v[6])
    w = [None, e + v[4], v[2] - v[6], e - v[4]]
    a, b = v[1] + v[7], v[3] + v[5]
    s, t = v[1] - v[7], v[3] - v[5]
    o = [None, c3 * a + c1 * b, r2 * (s + t), c1 * a - c3 * b]
    low = [o[k] + w[k] for k in range(1, 4)]
    high = [o[k] - w[k] for k in range(3, 0, -1)]
    return [None] + low + [s - t] + high


def split(x):
    high = x.astype(jnp.bfloat16)
    return high, (x - high.astype(jnp.float32)).astype(jnp.bfloat16)


def dot(a, b, rhs_dim=0):
    return lax.dot_general(
        a, b, (((1,), (rhs_dim,)), ((), ())), preferred_element_type=jnp.float32
    )


def send_order(owners):
    def hops(i):
        z, y = i // 8, i // 2 % 4
        return min(z, 4 - z) + min(y, 4 - y)

    return [0] + sorted(range(1, owners), key=lambda i: -hops(i))


def layout_tables(owners, cap, tiles):
    order = np.repeat(np.asarray(send_order(owners), np.int32)[:, None], tiles, axis=1)
    j, lane = np.arange(owners * cap)[:, None], np.arange(TP)[None, :]
    source = (j // cap == np.arange(TP)[None, :owners]).astype(jnp.bfloat16)
    entry = ((lane % FIELD == j % cap) & (lane < 3 * FIELD)).astype(np.float32)
    spread = (np.arange(TP)[:, None] // FIELD == np.arange(3 * TP)[None, :] // TP).astype(jnp.bfloat16)
    return order, source, entry, spread


def kernel(
    owners, cap, shots, shot_blocks, operand_count, *refs
):
    hbm, out_ref, rest = refs[:operand_count], refs[operand_count], refs[operand_count + 1 :]
    local, load_sem, rest = rest[:operand_count], rest[operand_count], rest[operand_count + 1 :]
    (
        owner_ref, place_ref, kind_ref, len_ref, order_ref, pix_ref,
        source_ref, entry_ref, spread_ref, weights_ref, turns_ref, dft_ref,
    ) = local
    (
        wide, send, recv, meta, meta_send, meta_recv, fields_col,
        is_kind, chosen, values, cycles, shares, high, low, spectra, inverse,
        send_sem, piece_sem, meta_send_sem, meta_recv_sem, halo_sem,
    ) = rest
    me, block = lax.axis_index("blk"), lax.axis_index("shot")
    tiles = owner_ref.shape[1]
    rows = cap * shots
    halo, mask = shots, shots + 1
    turned_back = shots + 2
    bf16, f32 = jnp.bfloat16, jnp.float32
    left = lax.rem(block + shot_blocks - 1, shot_blocks)
    right = lax.rem(block + 1, shot_blocks)
    order = send_order(owners)

    barrier = pltpu.get_barrier_semaphore()
    pl.semaphore_signal(barrier, inc=1, device_id=(right, me), device_id_type=MESH)
    for k in range(1, owners):
        pl.semaphore_signal(
            barrier,
            inc=1,
            device_id=(block, lax.bitwise_xor(me, order[k])),
            device_id_type=MESH,
        )

    loads = [
        pltpu.make_async_copy(source, target, load_sem.at[i])
        for i, (source, target) in enumerate(zip(hbm, local))
    ]
    for load in loads:
        load.start()

    for load in loads[:5]:
        load.wait()

    goes = order_ref[...] == lax.bitwise_xor(owner_ref[...], me)
    goes_bf = goes.astype(f32).astype(bf16)
    before = (
        lax.broadcasted_iota(jnp.int32, (tiles, tiles), 0)
        < lax.broadcasted_iota(jnp.int32, (tiles, tiles), 1)
    ).astype(f32).astype(bf16)
    number = lax.broadcasted_iota(jnp.int32, (owners, tiles), 0).astype(f32)
    earlier = dot(goes_bf, before)
    rank = jnp.sum(jnp.where(goes, earlier, 0.0), axis=0, keepdims=True)
    position = jnp.sum(jnp.where(goes, earlier + number * cap, 0.0), axis=0, keepdims=True)

    place = place_ref[...]
    place = lax.rem(place, NSEG) * Q_DEV + lax.div(place, NSEG)
    at_rank = lax.broadcasted_iota(jnp.int32, (FIELD, tiles), 0).astype(f32) == rank
    fields = [
        jnp.where(at_rank, jnp.broadcast_to(f.astype(f32), at_rank.shape), 0.0)
        for f in (place, kind_ref[...], len_ref[...])
    ]
    fields = jnp.concatenate(fields + [jnp.zeros((FIELD, tiles), f32)], axis=0).astype(bf16)
    meta[...] = dot(goes_bf, fields, 1)

    def lay_meta(i, carry):
        meta_send[i] = meta[pl.ds(i, 1), :]
        return carry

    lax.fori_loop(0, owners, lay_meta, 0)
    meta_recv[0] = meta_send[0]

    loads[5].wait()
    wide[...] = pix_ref[...].astype(f32)
    lengths = len_ref[...].astype(f32)
    lengths = jnp.concatenate(
        [
            jnp.transpose(jnp.broadcast_to(lengths[:, i : i + TP], (TP, TP)))
            for i in range(0, tiles, TP)
        ],
        axis=0,
    )
    live = lax.broadcasted_iota(jnp.int32, (tiles, TP), 1).astype(f32) < lengths
    masked = jnp.concatenate(
        [
            jnp.where(live, wide[pl.ds(s, tiles, stride=shots), :], 0.0).astype(bf16)
            for s in range(shots)
        ],
        axis=1,
    )

    def meta_copy(here, i):
        return pltpu.make_async_remote_copy(
            src_ref=meta_send.at[here], dst_ref=meta_recv.at[here],
            send_sem=meta_send_sem, recv_sem=meta_recv_sem,
            device_id=(block, lax.bitwise_xor(me, i)), device_id_type=MESH,
        )

    def pixel_copy(here, part, sem, i):
        return pltpu.make_async_remote_copy(
            src_ref=send.at[here, part], dst_ref=recv.at[here, part],
            send_sem=send_sem, recv_sem=sem,
            device_id=(block, lax.bitwise_xor(me, i)), device_id_type=MESH,
        )

    def group_of(k):
        return sum(k >= start for start in STARTS[1:-1])

    third = rows // 3
    pieces = [pl.ds(part * third, third) for part in range(3)]

    def pack(first, count):
        spot = lax.broadcasted_iota(jnp.int32, (count * cap, tiles), 0) + first * cap
        placing = (spot.astype(f32) == position).astype(f32).astype(bf16)
        packed = dot(placing, masked)
        for d in range(count):
            mine = packed[d * cap : (d + 1) * cap]
            mine = jnp.concatenate([mine[:, s * TP : (s + 1) * TP] for s in range(shots)], axis=0)
            send[first + d] = mine.astype(bf16)

    for first in range(0, owners, BATCH):
        pack(first, BATCH)
    recv[0] = send[0]

    pl.semaphore_wait(barrier, owners)
    for k in range(1, owners):
        meta_copy(k, order[k]).start()
    for part in range(2):
        for k in range(1, owners):
            pixel_copy(k, pieces[part], piece_sem.at[part], order[k]).start()
    for k in range(1, owners):
        pixel_copy(k, pieces[2], piece_sem.at[2 + group_of(k)], order[k]).start()

    others = pl.ds(1, owners - 1)
    for load in loads[6:10]:
        load.wait()
    meta_copy(others, 1).wait_recv()

    entries = dot(source_ref[...], meta_recv[...].reshape(owners, TP).astype(bf16))
    fields_col[...] = dot((entries * entry_ref[...]).astype(bf16), spread_ref[...])
    slots = Q_DEV * NSEG
    slot = lax.broadcasted_iota(jnp.int32, (slots, TP), 0).astype(f32)
    for i in range(owners * cap // TP):
        line = jnp.transpose(fields_col[i * TP : (i + 1) * TP, :TP])
        line = jnp.broadcast_to(line[0:1], (slots, TP))
        chosen[:, i * TP : (i + 1) * TP] = (slot == line).astype(f32).astype(bf16)

    kinds = weights_ref.shape[0]
    weights = weights_ref[...].reshape(kinds * TP, TP)

    def mark_kinds(i, carry):
        kind = fields_col[pl.ds(pl.multiple_of(i * cap, 8), cap), TP : 2 * TP]
        is_kind[i] = jnp.concatenate([kind] * shots, axis=0).astype(bf16)
        return carry

    def keep(here, column, product):
        hi, lo = split(product)
        values[here, 2 * column * TP : (2 * column + 1) * TP] = hi
        values[here, (2 * column + 1) * TP : (2 * column + 2) * TP] = lo

    def interpolate(first, count, start, end, first_shot, last_shot):
        here = pl.ds(pl.multiple_of(first * cap, 16), count * cap)
        size, these = end - start, pl.ds(first, count)
        pixels = recv[these, start:end].reshape(count * size, TP)
        kind = is_kind[these, start:end].reshape(count * size, TP)
        none = jnp.zeros_like(pixels)
        spread = [jnp.where(kind == jnp.asarray(k, bf16), pixels, none) for k in range(kinds)]
        product = dot(jnp.concatenate(spread, axis=1), weights)
        for s in range(first_shot, last_shot):
            mine = [
                product[i * size + s * cap - start : i * size + (s + 1) * cap - start]
                for i in range(count)
            ]
            keep(here, s, jnp.concatenate(mine, axis=0))

    def interpolate_live(g, carry):
        span = BATCH * cap
        here = pl.ds(pl.multiple_of(g * span, 16), span)
        pixel = lax.broadcasted_iota(jnp.int32, (span, TP), 1).astype(f32)
        kind = fields_col[here, TP : 2 * TP]
        alive = jnp.where(pixel < fields_col[here, 2 * TP :], kind, -1.0)
        spread = [(alive == float(k)).astype(f32).astype(bf16) for k in range(kinds)]
        keep(here, shots, dot(jnp.concatenate(spread, axis=1), weights))
        return carry

    lax.fori_loop(0, owners // BATCH, interpolate_live, 0)
    lax.fori_loop(0, owners, mark_kinds, 0)

    def gather(s, target, start=0, end=owners * cap):
        both = dot(chosen[:, start:end], values[start:end, 2 * s * TP : (2 * s + 2) * TP])
        both = both[:, :TP] + both[:, TP:]
        cycles[target] = both + cycles[target] if start else both

    gather(shots, mask)

    def put(here, real, imag):
        for j, part in enumerate((real, imag)):
            hi, lo = split(part)
            high[here, j * TP : (j + 1) * TP] = hi
            low[here, j * TP : (j + 1) * TP] = lo

    def band(s, k):
        return pl.ds(pl.multiple_of(s * ROWS + k * Q_DEV, 16), Q_DEV)

    def forward(s):
        x = [cycles[s, a * Q_DEV : (a + 1) * Q_DEV, :] for a in range(NSEG)]
        total = [None] + [x[a] + x[NSEG - a] for a in range(1, HALF)]
        differ = [None] + [x[a] - x[NSEG - a] for a in range(1, HALF)]
        real = cosine_sums(x[0], x[HALF], total)
        imag = sine_sums(differ)
        for k in range(FREQS):
            here = band(s, k)
            cos, sin = turns_ref[0, k : k + 1, :], turns_ref[1, k : k + 1, :]
            if k == 0:
                put(here, real[k], jnp.zeros_like(real[k]))
            elif k == HALF:
                put(here, real[k] * cos, real[k] * sin)
            else:
                put(here, real[k] * cos + imag[k] * sin, real[k] * sin - imag[k] * cos)

    def transform(result, target, first, count):
        here = pl.ds(first * ROWS, count * ROWS)
        hi, lo = high[here, :], low[here, :]
        found = dot(jnp.concatenate([hi, lo, hi], axis=1), dft_ref[...])
        result[pl.ds(target * ROWS, count * ROWS), :] = found

    def correlate(s, following, target):
        for k in range(FREQS):
            mine = spectra[band(s, k), :]
            xr, xi = mine[:, :TP], mine[:, TP:]
            if following is None:
                put(band(target, k), xr * xr + xi * xi, jnp.zeros_like(xr))
            else:
                differ = mine - spectra[band(following, k), :]
                dr, di = differ[:, :TP], differ[:, TP:]
                put(band(target, k), xr * dr + xi * di, xr * di - xi * dr)

    def back(s):
        parts = []
        for k in range(FREQS):
            here = band(s, k)
            re, im = inverse[here, :TP], inverse[here, TP:]
            cos, sin = turns_ref[2, k : k + 1, :], turns_ref[3, k : k + 1, :]
            parts.append((re * cos - im * sin, re * sin + im * cos))
        sums = cosine_sums(parts[0][0], parts[HALF][0], [p[0] for p in parts])
        turned = sine_sums([p[1] for p in parts])
        found = [None] * NSEG
        found[0], found[HALF] = sums[0], sums[HALF]
        for a in range(1, HALF):
            found[a], found[NSEG - a] = sums[a] + turned[a], sums[a] - turned[a]
        return found

    for load in loads[10:]:
        load.wait()
    forward(mask)
    transform(spectra, mask, mask, 1)
    correlate(mask, None, turned_back + shots)
    transform(inverse, shots, turned_back + shots, 1)
    overlap = back(shots)
    floor = jnp.maximum(0.01 * overlap[0][:, 0:1], 1.0)
    for a in range(NSEG):
        shares[a * Q_DEV : (a + 1) * Q_DEV, :] = 1.0 / jnp.maximum(overlap[a], floor)

    def finish(s):
        found = back(s)
        for a in range(NSEG):
            share = shares[a * Q_DEV : (a + 1) * Q_DEV, :]
            out_ref[s, :, a * TP : (a + 1) * TP] = found[a] * share

    pixel_copy(others, pieces[0], piece_sem.at[0], 1).wait_recv()
    for first in range(0, owners, BATCH):
        interpolate(first, BATCH, 0, third, 0, 1)
    gather(0, 0)
    halo_copy = pltpu.make_async_remote_copy(
        src_ref=cycles.at[0], dst_ref=cycles.at[halo],
        send_sem=halo_sem.at[0], recv_sem=halo_sem.at[1],
        device_id=(left, me), device_id_type=MESH,
    )
    halo_copy.start()
    forward(0)
    transform(spectra, 0, 0, 1)

    pixel_copy(others, pieces[1], piece_sem.at[1], 1).wait_recv()
    for first in range(0, owners, BATCH):
        interpolate(first, BATCH, 16, 48, 1, 2)
    gather(1, 1)
    forward(1)
    transform(spectra, 1, 1, 1)
    correlate(0, 1, turned_back)
    transform(inverse, 0, turned_back, 1)
    finish(0)

    def take_group(g):
        skip = 1 if g == 0 else 0
        pixel_copy(
            pl.ds(STARTS[g] + skip, STARTS[g + 1] - STARTS[g] - skip),
            pieces[2],
            piece_sem.at[2 + g],
            1,
        ).wait_recv()
        interpolate(STARTS[g], STARTS[g + 1] - STARTS[g], 48, rows, 2, shots)

    groups = len(STARTS) - 1
    early = STARTS[groups - LATE] * cap
    for g in range(groups - LATE):
        take_group(g)
    for s in range(2, shots):
        gather(s, s, 0, early)
    for g in range(groups - LATE, groups):
        take_group(g)
    for s in range(2, shots):
        gather(s, s, early, owners * cap)
        forward(s)
    halo_copy.wait_recv()
    forward(halo)
    for s in range(2, shots + 1):
        transform(spectra, s, s, 1)
    for s in range(1, shots):
        correlate(s, s + 1, turned_back + s)
        transform(inverse, s, turned_back + s, 1)
    for s in range(1, shots):
        finish(s)

    halo_copy.wait_send()
    meta_copy(others, 1).wait_send()
    pixel_copy(others, pl.ds(0, rows), piece_sem.at[0], 1).wait_send()


def per_device(intensities, tile_owner, tile_place, tile_kernel, mask_len, interp_weights):
    owners, shot_blocks = lax.axis_size("blk"), lax.axis_size("shot")
    tiles, shots, _ = intensities.shape
    cap = 3 * tiles // owners
    dft, turns = dft_tables()
    order, source, entry, spread = layout_tables(owners, cap, tiles)
    bf16, f32 = jnp.bfloat16, jnp.float32
    slots = Q_DEV * NSEG
    operands = (
        tile_owner.reshape(1, tiles),
        tile_place.reshape(1, tiles),
        tile_kernel.reshape(1, tiles),
        mask_len.reshape(1, tiles),
        jnp.asarray(order),
        intensities.reshape(tiles * shots, TP),
        jnp.asarray(source),
        jnp.asarray(entry),
        jnp.asarray(spread),
        interp_weights,
        jnp.asarray(turns),
        jnp.asarray(dft),
    )
    return pl.pallas_call(
        functools.partial(kernel, owners, cap, shots, shot_blocks, len(operands)),
        out_shape=jax.ShapeDtypeStruct((shots, Q_DEV, ANG), f32),
        in_specs=[pl.BlockSpec(memory_space=pltpu.HBM)] * len(operands),
        out_specs=pl.BlockSpec(memory_space=pltpu.VMEM),
        scratch_shapes=[pltpu.VMEM(x.shape, x.dtype) for x in operands]
        + [pltpu.SemaphoreType.DMA((len(operands),))]
        + [
            pltpu.VMEM((tiles * shots, TP), f32),
            pltpu.VMEM((owners, cap * shots, TP), bf16),
            pltpu.VMEM((owners, cap * shots, TP), bf16),
            pltpu.VMEM((owners, TP), f32),
            pltpu.VMEM((owners, 1, TP), f32),
            pltpu.VMEM((owners, 1, TP), f32),
            pltpu.VMEM((owners * cap, 3 * TP), f32),
            pltpu.VMEM((owners, cap * shots, TP), bf16),
            pltpu.VMEM((slots, owners * cap), bf16),
            pltpu.VMEM((owners * cap, (shots + 1) * 2 * TP), bf16),
            pltpu.VMEM((shots + 2, slots, TP), f32),
            pltpu.VMEM((slots, TP), f32),
            pltpu.VMEM(((2 * shots + 3) * ROWS, 2 * TP), bf16),
            pltpu.VMEM(((2 * shots + 3) * ROWS, 2 * TP), bf16),
            pltpu.VMEM(((shots + 2) * ROWS, 2 * TP), f32),
            pltpu.VMEM(((shots + 1) * ROWS, 2 * TP), f32),
            pltpu.SemaphoreType.DMA,
            pltpu.SemaphoreType.DMA((len(STARTS) + 1,)),
            pltpu.SemaphoreType.DMA,
            pltpu.SemaphoreType.DMA,
            pltpu.SemaphoreType.DMA((2,)),
        ],
        compiler_params=pltpu.CompilerParams(
            collective_id=0, has_side_effects=True, vmem_limit_bytes=40 * 2**20
        ),
        cost_estimate=pl.CostEstimate(
            flops=3 * 10**9, bytes_accessed=2 * 10**6, transcendentals=0
        ),
    )(*(pltpu.with_memory_space_constraint(x, pltpu.HBM) for x in operands))


def solution(mesh):
    placed = (P("blk", "shot", None), P("blk"), P("blk"), P("blk"), P("blk"), P())
    return jax.shard_map(
        per_device, mesh=mesh, in_specs=placed, out_specs=P("shot", "blk", None), check_vma=False
    )
```

```python
import functools
import math

import jax
import jax.numpy as jnp
import numpy as np
from jax import lax
from jax.experimental import pallas as pl
from jax.experimental.pallas import tpu as pltpu
from jax.sharding import PartitionSpec as P

ANG = 2048
TP = 128
Q_DEV = 16
NSEG = 16
HALF = NSEG // 2
FREQS = HALF + 1
ROWS = FREQS * Q_DEV
FIELD = 32
STARTS = (0, 16, 32)
BATCH = 16
LATE = 1
MESH = pl.DeviceIdType.MESH


def dft_tables():
    b = np.arange(TP)
    angle = 2.0 * math.pi * (np.outer(b, b) % TP) / TP
    cos, sin = np.cos(angle), np.sin(angle)
    table = np.block([[cos, -sin], [sin, cos]]).astype(np.float32)
    high = table.astype(jnp.bfloat16)
    low = (table - high.astype(np.float32)).astype(jnp.bfloat16)
    dft = np.concatenate([high, high, low], axis=0)
    twist = 2.0 * math.pi * (np.outer(np.arange(FREQS), b) % ANG) / ANG
    scale = np.full((FREQS, 1), 2.0 / ANG)
    scale[0] = scale[HALF] = 1.0 / ANG
    turns = np.stack(
        [np.cos(twist), -np.sin(twist), scale * np.cos(twist), -scale * np.sin(twist)]
    ).astype(np.float32)
    return dft, turns


def cosine_sums(first, middle, rest):
    c1, c3, r2 = math.cos(math.pi / 8), math.cos(3 * math.pi / 8), math.sqrt(0.5)
    even, odd = first + middle, first - middle
    g, h = rest[2] + rest[6], r2 * (rest[2] - rest[6])
    base = even + rest[4]
    p = [base + g, odd + h, even - rest[4], odd - h, base - g]
    u1, u3 = rest[1] - rest[7], rest[3] - rest[5]
    t1, t3 = rest[1] + rest[7], rest[3] + rest[5]
    q = [t1 + t3, c1 * u1 + c3 * u3, r2 * (t1 - t3), c3 * u1 - c1 * u3]
    low = [p[k] + q[k] for k in range(4)]
    high = [p[k] - q[k] for k in range(3, -1, -1)]
    return low + [p[4]] + high


def sine_sums(v):
    c1, c3, r2 = math.cos(math.pi / 8), math.cos(3 * math.pi / 8), math.sqrt(0.5)
    e = r2 * (v[2] + v[6])
    w = [None, e + v[4], v[2] - v[6], e - v[4]]
    a, b = v[1] + v[7], v[3] + v[5]
    s, t = v[1] - v[7], v[3] - v[5]
    o = [None, c3 * a + c1 * b, r2 * (s + t), c1 * a - c3 * b]
    low = [o[k] + w[k] for k in range(1, 4)]
    high = [o[k] - w[k] for k in range(3, 0, -1)]
    return [None] + low + [s - t] + high


def split(x):
    high = x.astype(jnp.bfloat16)
    return high, (x - high.astype(jnp.float32)).astype(jnp.bfloat16)


def dot(a, b, rhs_dim=0):
    return lax.dot_general(
        a, b, (((1,), (rhs_dim,)), ((), ())), preferred_element_type=jnp.float32
    )


def send_order(owners):
    def hops(i):
        z, y = i // 8, i // 2 % 4
        return min(z, 4 - z) + min(y, 4 - y)

    return [0] + sorted(range(1, owners), key=lambda i: -hops(i))


def layout_tables(owners, cap, tiles):
    order = np.repeat(np.asarray(send_order(owners), np.int32)[:, None], tiles, axis=1)
    j, lane = np.arange(owners * cap)[:, None], np.arange(TP)[None, :]
    source = (j // cap == np.arange(TP)[None, :owners]).astype(jnp.bfloat16)
    entry = ((lane % FIELD == j % cap) & (lane < 3 * FIELD)).astype(np.float32)
    spread = (np.arange(TP)[:, None] // FIELD == np.arange(3 * TP)[None, :] // TP).astype(jnp.bfloat16)
    return order, source, entry, spread


def kernel(
    owners, cap, shots, shot_blocks, operand_count, *refs
):
    hbm, out_ref, rest = refs[:operand_count], refs[operand_count], refs[operand_count + 1 :]
    local, load_sem, rest = rest[:operand_count], rest[operand_count], rest[operand_count + 1 :]
    (
        owner_ref, place_ref, kind_ref, len_ref, order_ref, pix_ref,
        source_ref, entry_ref, spread_ref, weights_ref, turns_ref, dft_ref,
    ) = local
    (
        wide, send, recv, meta, meta_send, meta_recv, fields_col,
        is_kind, chosen, values, cycles, shares, high, low, spectra, inverse,
        send_sem, piece_sem, meta_send_sem, meta_recv_sem, halo_sem,
    ) = rest
    me, block = lax.axis_index("blk"), lax.axis_index("shot")
    tiles = owner_ref.shape[1]
    rows = cap * shots
    halo, mask = shots, shots + 1
    turned_back = shots + 2
    bf16, f32 = jnp.bfloat16, jnp.float32
    left = lax.rem(block + shot_blocks - 1, shot_blocks)
    right = lax.rem(block + 1, shot_blocks)
    order = send_order(owners)

    barrier = pltpu.get_barrier_semaphore()
    pl.semaphore_signal(barrier, inc=1, device_id=(right, me), device_id_type=MESH)
    for k in range(1, owners):
        pl.semaphore_signal(
            barrier,
            inc=1,
            device_id=(block, lax.bitwise_xor(me, order[k])),
            device_id_type=MESH,
        )

    loads = [
        pltpu.make_async_copy(source, target, load_sem.at[i])
        for i, (source, target) in enumerate(zip(hbm, local))
    ]
    for load in loads:
        load.start()

    for load in loads[:5]:
        load.wait()

    goes = order_ref[...] == lax.bitwise_xor(owner_ref[...], me)
    goes_bf = goes.astype(f32).astype(bf16)
    before = (
        lax.broadcasted_iota(jnp.int32, (tiles, tiles), 0)
        < lax.broadcasted_iota(jnp.int32, (tiles, tiles), 1)
    ).astype(f32).astype(bf16)
    number = lax.broadcasted_iota(jnp.int32, (owners, tiles), 0).astype(f32)
    earlier = dot(goes_bf, before)
    rank = jnp.sum(jnp.where(goes, earlier, 0.0), axis=0, keepdims=True)
    position = jnp.sum(jnp.where(goes, earlier + number * cap, 0.0), axis=0, keepdims=True)

    place = place_ref[...]
    place = lax.rem(place, NSEG) * Q_DEV + lax.div(place, NSEG)
    at_rank = lax.broadcasted_iota(jnp.int32, (FIELD, tiles), 0).astype(f32) == rank
    fields = [
        jnp.where(at_rank, jnp.broadcast_to(f.astype(f32), at_rank.shape), 0.0)
        for f in (place, kind_ref[...], len_ref[...])
    ]
    fields = jnp.concatenate(fields + [jnp.zeros((FIELD, tiles), f32)], axis=0).astype(bf16)
    meta[...] = dot(goes_bf, fields, 1)

    def lay_meta(i, carry):
        meta_send[i] = meta[pl.ds(i, 1), :]
        return carry

    lax.fori_loop(0, owners, lay_meta, 0)
    meta_recv[0] = meta_send[0]

    loads[5].wait()
    wide[0 : tiles * shots, :] = pix_ref[...].astype(f32)
    lengths = len_ref[...].astype(f32)
    lengths = jnp.concatenate(
        [
            jnp.transpose(jnp.broadcast_to(lengths[:, i : i + TP], (TP, TP)))
            for i in range(0, tiles, TP)
        ],
        axis=0,
    )
    live = lax.broadcasted_iota(jnp.int32, (tiles, TP), 1).astype(f32) < lengths
    masked = jnp.concatenate(
        [
            jnp.where(live, wide[pl.ds(s, tiles, stride=shots), :], 0.0).astype(bf16)
            for s in range(shots)
        ],
        axis=1,
    )

    def meta_copy(here, i):
        return pltpu.make_async_remote_copy(
            src_ref=meta_send.at[here], dst_ref=meta_recv.at[here],
            send_sem=meta_send_sem, recv_sem=meta_recv_sem,
            device_id=(block, lax.bitwise_xor(me, i)), device_id_type=MESH,
        )

    def pixel_copy(here, part, sem, i):
        return pltpu.make_async_remote_copy(
            src_ref=send.at[here, part], dst_ref=recv.at[here, part],
            send_sem=send_sem, recv_sem=sem,
            device_id=(block, lax.bitwise_xor(me, i)), device_id_type=MESH,
        )

    def group_of(k):
        return sum(k >= start for start in STARTS[1:-1])

    third = rows // 3
    pieces = [pl.ds(part * third, third) for part in range(3)]

    def pack(first, count):
        spot = lax.broadcasted_iota(jnp.int32, (count * cap, tiles), 0) + first * cap
        placing = (spot.astype(f32) == position).astype(f32).astype(bf16)
        packed = dot(placing, masked)
        for d in range(count):
            mine = packed[d * cap : (d + 1) * cap]
            mine = jnp.concatenate([mine[:, s * TP : (s + 1) * TP] for s in range(shots)], axis=0)
            send[first + d] = mine.astype(bf16)

    for first in range(0, owners, BATCH):
        pack(first, BATCH)
    recv[0] = send[0]

    pl.semaphore_wait(barrier, owners)
    for k in range(1, owners):
        meta_copy(k, order[k]).start()
    for part in range(2):
        for k in range(1, owners):
            pixel_copy(k, pieces[part], piece_sem.at[part], order[k]).start()
    for k in range(1, owners):
        pixel_copy(k, pieces[2], piece_sem.at[2 + group_of(k)], order[k]).start()

    others = pl.ds(1, owners - 1)
    for load in loads[6:10]:
        load.wait()
    meta_copy(others, 1).wait_recv()

    entries = dot(source_ref[...], meta_recv[...].reshape(owners, TP).astype(bf16))
    fields_col[...] = dot((entries * entry_ref[...]).astype(bf16), spread_ref[...])
    slots = Q_DEV * NSEG
    slot = lax.broadcasted_iota(jnp.int32, (slots, TP), 0).astype(f32)
    for i in range(owners * cap // TP):
        line = jnp.transpose(fields_col[i * TP : (i + 1) * TP, :TP])
        line = jnp.broadcast_to(line[0:1], (slots, TP))
        chosen[:, i * TP : (i + 1) * TP] = (slot == line).astype(f32).astype(bf16)

    kinds = weights_ref.shape[0]
    weights = weights_ref[...].reshape(kinds * TP, TP)

    def mark_kinds(i, carry):
        kind = fields_col[pl.ds(pl.multiple_of(i * cap, 8), cap), TP : 2 * TP]
        is_kind[i] = jnp.concatenate([kind] * shots, axis=0).astype(bf16)
        return carry

    def keep(here, column, product):
        hi, lo = split(product)
        values[here, 2 * column * TP : (2 * column + 1) * TP] = hi
        values[here, (2 * column + 1) * TP : (2 * column + 2) * TP] = lo

    def interpolate(first, count, start, end, first_shot, last_shot):
        here = pl.ds(pl.multiple_of(first * cap, 16), count * cap)
        size, these = end - start, pl.ds(first, count)
        pixels = recv[these, start:end].reshape(count * size, TP)
        kind = is_kind[these, start:end].reshape(count * size, TP)
        none = jnp.zeros_like(pixels)
        spread = [jnp.where(kind == jnp.asarray(k, bf16), pixels, none) for k in range(kinds)]
        product = dot(jnp.concatenate(spread, axis=1), weights)
        for s in range(first_shot, last_shot):
            mine = [
                product[i * size + s * cap - start : i * size + (s + 1) * cap - start]
                for i in range(count)
            ]
            keep(here, s, jnp.concatenate(mine, axis=0))

    def interpolate_live(g, carry):
        span = BATCH * cap
        here = pl.ds(pl.multiple_of(g * span, 16), span)
        pixel = lax.broadcasted_iota(jnp.int32, (span, TP), 1).astype(f32)
        kind = fields_col[here, TP : 2 * TP]
        alive = jnp.where(pixel < fields_col[here, 2 * TP :], kind, -1.0)
        spread = [(alive == float(k)).astype(f32).astype(bf16) for k in range(kinds)]
        keep(here, shots, dot(jnp.concatenate(spread, axis=1), weights))
        return carry

    lax.fori_loop(0, owners // BATCH, interpolate_live, 0)
    lax.fori_loop(0, owners, mark_kinds, 0)

    def gather(s, target, start=0, end=owners * cap):
        both = dot(chosen[:, start:end], values[start:end, 2 * s * TP : (2 * s + 2) * TP])
        both = both[:, :TP] + both[:, TP:]
        cycles[target] = both + cycles[target] if start else both

    gather(shots, mask)

    def put(here, real, imag):
        for j, part in enumerate((real, imag)):
            hi, lo = split(part)
            high[here, j * TP : (j + 1) * TP] = hi
            low[here, j * TP : (j + 1) * TP] = lo

    def band(s, k):
        return pl.ds(pl.multiple_of(s * ROWS + k * Q_DEV, 16), Q_DEV)

    def forward(s):
        x = [cycles[s, a * Q_DEV : (a + 1) * Q_DEV, :] for a in range(NSEG)]
        total = [None] + [x[a] + x[NSEG - a] for a in range(1, HALF)]
        differ = [None] + [x[a] - x[NSEG - a] for a in range(1, HALF)]
        real = cosine_sums(x[0], x[HALF], total)
        imag = sine_sums(differ)
        for k in range(FREQS):
            here = band(s, k)
            cos, sin = turns_ref[0, k : k + 1, :], turns_ref[1, k : k + 1, :]
            if k == 0:
                put(here, real[k], jnp.zeros_like(real[k]))
            elif k == HALF:
                put(here, real[k] * cos, real[k] * sin)
            else:
                put(here, real[k] * cos + imag[k] * sin, real[k] * sin - imag[k] * cos)

    def transform(result, target, first, count):
        here = pl.ds(first * ROWS, count * ROWS)
        hi, lo = high[here, :], low[here, :]
        found = dot(jnp.concatenate([hi, lo, hi], axis=1), dft_ref[...])
        result[pl.ds(target * ROWS, count * ROWS), :] = found

    def correlate(s, following, target):
        for k in range(FREQS):
            mine = spectra[band(s, k), :]
            xr, xi = mine[:, :TP], mine[:, TP:]
            if following is None:
                put(band(target, k), xr * xr + xi * xi, jnp.zeros_like(xr))
            else:
                differ = mine - spectra[band(following, k), :]
                dr, di = differ[:, :TP], differ[:, TP:]
                put(band(target, k), xr * dr + xi * di, xr * di - xi * dr)

    def back(s):
        parts = []
        for k in range(FREQS):
            here = band(s, k)
            re, im = inverse[here, :TP], inverse[here, TP:]
            cos, sin = turns_ref[2, k : k + 1, :], turns_ref[3, k : k + 1, :]
            parts.append((re * cos - im * sin, re * sin + im * cos))
        sums = cosine_sums(parts[0][0], parts[HALF][0], [p[0] for p in parts])
        turned = sine_sums([p[1] for p in parts])
        found = [None] * NSEG
        found[0], found[HALF] = sums[0], sums[HALF]
        for a in range(1, HALF):
            found[a], found[NSEG - a] = sums[a] + turned[a], sums[a] - turned[a]
        return found

    for load in loads[10:]:
        load.wait()
    forward(mask)
    transform(spectra, mask, mask, 1)
    correlate(mask, None, turned_back + shots)
    transform(inverse, shots, turned_back + shots, 1)
    overlap = back(shots)
    floor = jnp.maximum(0.01 * overlap[0][:, 0:1], 1.0)
    for a in range(NSEG):
        shares[a * Q_DEV : (a + 1) * Q_DEV, :] = 1.0 / jnp.maximum(overlap[a], floor)

    def finish(s):
        found = back(s)
        for a in range(NSEG):
            share = shares[a * Q_DEV : (a + 1) * Q_DEV, :]
            out_ref[s, :, a * TP : (a + 1) * TP] = found[a] * share

    pixel_copy(others, pieces[0], piece_sem.at[0], 1).wait_recv()
    for first in range(0, owners, BATCH):
        interpolate(first, BATCH, 0, third, 0, 1)
    gather(0, 0)
    halo_copy = pltpu.make_async_remote_copy(
        src_ref=cycles.at[0], dst_ref=cycles.at[halo],
        send_sem=halo_sem.at[0], recv_sem=halo_sem.at[1],
        device_id=(left, me), device_id_type=MESH,
    )
    halo_copy.start()
    forward(0)
    transform(spectra, 0, 0, 1)

    pixel_copy(others, pieces[1], piece_sem.at[1], 1).wait_recv()
    for first in range(0, owners, BATCH):
        interpolate(first, BATCH, 16, 48, 1, 2)
    gather(1, 1)
    forward(1)
    transform(spectra, 1, 1, 1)
    correlate(0, 1, turned_back)
    transform(inverse, 0, turned_back, 1)
    finish(0)

    def take_group(g):
        skip = 1 if g == 0 else 0
        pixel_copy(
            pl.ds(STARTS[g] + skip, STARTS[g + 1] - STARTS[g] - skip),
            pieces[2],
            piece_sem.at[2 + g],
            1,
        ).wait_recv()
        interpolate(STARTS[g], STARTS[g + 1] - STARTS[g], 48, rows, 2, shots)

    groups = len(STARTS) - 1
    early = STARTS[groups - LATE] * cap
    for g in range(groups - LATE):
        take_group(g)
    for s in range(2, shots):
        gather(s, s, 0, early)
    for g in range(groups - LATE, groups):
        take_group(g)
    for s in range(2, shots):
        gather(s, s, early, owners * cap)
        forward(s)
    halo_copy.wait_recv()
    forward(halo)
    for s in range(2, shots + 1):
        transform(spectra, s, s, 1)
    for s in range(1, shots):
        correlate(s, s + 1, turned_back + s)
        transform(inverse, s, turned_back + s, 1)
    for s in range(1, shots):
        finish(s)

    halo_copy.wait_send()
    meta_copy(others, 1).wait_send()
    pixel_copy(others, pl.ds(0, rows), piece_sem.at[0], 1).wait_send()


def per_device(intensities, tile_owner, tile_place, tile_kernel, mask_len, interp_weights):
    owners, shot_blocks = lax.axis_size("blk"), lax.axis_size("shot")
    tiles, shots, _ = intensities.shape
    cap = 3 * tiles // owners
    dft, turns = dft_tables()
    order, source, entry, spread = layout_tables(owners, cap, tiles)
    bf16, f32 = jnp.bfloat16, jnp.float32
    slots = Q_DEV * NSEG
    operands = (
        tile_owner.reshape(1, tiles),
        tile_place.reshape(1, tiles),
        tile_kernel.reshape(1, tiles),
        mask_len.reshape(1, tiles),
        jnp.asarray(order),
        intensities.reshape(tiles * shots, TP),
        jnp.asarray(source),
        jnp.asarray(entry),
        jnp.asarray(spread),
        interp_weights,
        jnp.asarray(turns),
        jnp.asarray(dft),
    )
    return pl.pallas_call(
        functools.partial(kernel, owners, cap, shots, shot_blocks, len(operands)),
        out_shape=jax.ShapeDtypeStruct((shots, Q_DEV, ANG), f32),
        in_specs=[pl.BlockSpec(memory_space=pltpu.HBM)] * len(operands),
        out_specs=pl.BlockSpec(memory_space=pltpu.VMEM),
        scratch_shapes=[pltpu.VMEM(x.shape, x.dtype) for x in operands]
        + [pltpu.SemaphoreType.DMA((len(operands),))]
        + [
            pltpu.VMEM(((tiles + Q_DEV) * shots, TP), f32),
            pltpu.VMEM((owners, cap * shots, TP), bf16),
            pltpu.VMEM((owners, cap * shots, TP), bf16),
            pltpu.VMEM((owners, TP), f32),
            pltpu.VMEM((owners, 1, TP), f32),
            pltpu.VMEM((owners, 1, TP), f32),
            pltpu.VMEM((owners * cap, 3 * TP), f32),
            pltpu.VMEM((owners, cap * shots, TP), bf16),
            pltpu.VMEM((slots, owners * cap), bf16),
            pltpu.VMEM((owners * cap, (shots + 1) * 2 * TP), bf16),
            pltpu.VMEM((shots + 2, slots, TP), f32),
            pltpu.VMEM((slots, TP), f32),
            pltpu.VMEM(((2 * shots + 3) * ROWS, 2 * TP), bf16),
            pltpu.VMEM(((2 * shots + 3) * ROWS, 2 * TP), bf16),
            pltpu.VMEM(((shots + 2) * ROWS, 2 * TP), f32),
            pltpu.VMEM(((shots + 1) * ROWS, 2 * TP), f32),
            pltpu.SemaphoreType.DMA,
            pltpu.SemaphoreType.DMA((len(STARTS) + 1,)),
            pltpu.SemaphoreType.DMA,
            pltpu.SemaphoreType.DMA,
            pltpu.SemaphoreType.DMA((2,)),
        ],
        compiler_params=pltpu.CompilerParams(
            collective_id=0, has_side_effects=True, vmem_limit_bytes=40 * 2**20
        ),
        cost_estimate=pl.CostEstimate(
            flops=3 * 10**9, bytes_accessed=2 * 10**6, transcendentals=0
        ),
    )(*(pltpu.with_memory_space_constraint(x, pltpu.HBM) for x in operands))


def solution(mesh):
    placed = (P("blk", "shot", None), P("blk"), P("blk"), P("blk"), P("blk"), P())
    return jax.shard_map(
        per_device, mesh=mesh, in_specs=placed, out_specs=P("shot", "blk", None), check_vma=False
    )
```

```python
import functools
import math

import jax
import jax.numpy as jnp
import numpy as np
from jax import lax
from jax.experimental import pallas as pl
from jax.experimental.pallas import tpu as pltpu
from jax.sharding import PartitionSpec as P

ANG = 2048
TP = 128
Q_DEV = 16
NSEG = 16
HALF = NSEG // 2
FREQS = HALF + 1
ROWS = FREQS * Q_DEV
FIELD = 32
STARTS = (0, 16, 32)
BATCH = 16
LATE = 1
MESH = pl.DeviceIdType.MESH


def dft_tables():
    b = np.arange(TP)
    angle = 2.0 * math.pi * (np.outer(b, b) % TP) / TP
    cos, sin = np.cos(angle), np.sin(angle)
    table = np.block([[cos, -sin], [sin, cos]]).astype(np.float32)
    high = table.astype(jnp.bfloat16)
    low = (table - high.astype(np.float32)).astype(jnp.bfloat16)
    dft = np.concatenate([high, high, low], axis=0)
    twist = 2.0 * math.pi * (np.outer(np.arange(FREQS), b) % ANG) / ANG
    scale = np.full((FREQS, 1), 2.0 / ANG)
    scale[0] = scale[HALF] = 1.0 / ANG
    turns = np.stack(
        [np.cos(twist), -np.sin(twist), scale * np.cos(twist), -scale * np.sin(twist)]
    ).astype(np.float32)
    return dft, turns


def cosine_sums(first, middle, rest):
    c1, c3, r2 = math.cos(math.pi / 8), math.cos(3 * math.pi / 8), math.sqrt(0.5)
    even, odd = first + middle, first - middle
    g, h = rest[2] + rest[6], r2 * (rest[2] - rest[6])
    base = even + rest[4]
    p = [base + g, odd + h, even - rest[4], odd - h, base - g]
    u1, u3 = rest[1] - rest[7], rest[3] - rest[5]
    t1, t3 = rest[1] + rest[7], rest[3] + rest[5]
    q = [t1 + t3, c1 * u1 + c3 * u3, r2 * (t1 - t3), c3 * u1 - c1 * u3]
    low = [p[k] + q[k] for k in range(4)]
    high = [p[k] - q[k] for k in range(3, -1, -1)]
    return low + [p[4]] + high


def sine_sums(v):
    c1, c3, r2 = math.cos(math.pi / 8), math.cos(3 * math.pi / 8), math.sqrt(0.5)
    e = r2 * (v[2] + v[6])
    w = [None, e + v[4], v[2] - v[6], e - v[4]]
    a, b = v[1] + v[7], v[3] + v[5]
    s, t = v[1] - v[7], v[3] - v[5]
    o = [None, c3 * a + c1 * b, r2 * (s + t), c1 * a - c3 * b]
    low = [o[k] + w[k] for k in range(1, 4)]
    high = [o[k] - w[k] for k in range(3, 0, -1)]
    return [None] + low + [s - t] + high


def split(x):
    high = x.astype(jnp.bfloat16)
    return high, (x - high.astype(jnp.float32)).astype(jnp.bfloat16)


def dot(a, b, rhs_dim=0):
    return lax.dot_general(
        a, b, (((1,), (rhs_dim,)), ((), ())), preferred_element_type=jnp.float32
    )


def send_order(owners):
    def hops(i):
        z, y = i // 8, i // 2 % 4
        return min(z, 4 - z) + min(y, 4 - y)

    return [0] + sorted(range(1, owners), key=lambda i: -hops(i))


def layout_tables(owners, cap, tiles):
    order = np.repeat(np.asarray(send_order(owners), np.int32)[:, None], tiles, axis=1)
    j, lane = np.arange(owners * cap)[:, None], np.arange(TP)[None, :]
    source = (j // cap == np.arange(TP)[None, :owners]).astype(jnp.bfloat16)
    entry = ((lane % FIELD == j % cap) & (lane < 3 * FIELD)).astype(np.float32)
    spread = (np.arange(TP)[:, None] // FIELD == np.arange(3 * TP)[None, :] // TP).astype(jnp.bfloat16)
    return order, source, entry, spread


def kernel(
    owners, cap, shots, shot_blocks, operand_count, *refs
):
    hbm, out_ref, rest = refs[:operand_count], refs[operand_count], refs[operand_count + 1 :]
    local, load_sem, rest = rest[:operand_count], rest[operand_count], rest[operand_count + 1 :]
    (
        owner_ref, place_ref, kind_ref, len_ref, order_ref, pix_ref,
        source_ref, entry_ref, spread_ref, weights_ref, turns_ref, dft_ref,
    ) = local
    (
        wide, send, recv, meta, meta_send, meta_recv, fields_col,
        is_kind, chosen, values, cycles, shares, high, low, spectra, inverse,
        send_sem, piece_sem, meta_send_sem, meta_recv_sem, halo_sem,
    ) = rest
    me, block = lax.axis_index("blk"), lax.axis_index("shot")
    tiles = owner_ref.shape[1]
    rows = cap * shots
    halo, mask = shots, shots + 1
    turned_back = shots + 2
    bf16, f32 = jnp.bfloat16, jnp.float32
    left = lax.rem(block + shot_blocks - 1, shot_blocks)
    right = lax.rem(block + 1, shot_blocks)
    order = send_order(owners)

    barrier = pltpu.get_barrier_semaphore()
    pl.semaphore_signal(barrier, inc=1, device_id=(right, me), device_id_type=MESH)
    for k in range(1, owners):
        pl.semaphore_signal(
            barrier,
            inc=1,
            device_id=(block, lax.bitwise_xor(me, order[k])),
            device_id_type=MESH,
        )

    loads = [
        pltpu.make_async_copy(source, target, load_sem.at[i])
        for i, (source, target) in enumerate(zip(hbm, local))
    ]
    for load in loads:
        load.start()

    for load in loads[:5]:
        load.wait()

    goes = order_ref[...] == lax.bitwise_xor(owner_ref[...], me)
    goes_bf = goes.astype(f32).astype(bf16)
    before = (
        lax.broadcasted_iota(jnp.int32, (tiles, tiles), 0)
        < lax.broadcasted_iota(jnp.int32, (tiles, tiles), 1)
    ).astype(f32).astype(bf16)
    number = lax.broadcasted_iota(jnp.int32, (owners, tiles), 0).astype(f32)
    earlier = dot(goes_bf, before)
    rank = jnp.sum(jnp.where(goes, earlier, 0.0), axis=0, keepdims=True)
    position = jnp.sum(jnp.where(goes, earlier + number * cap, 0.0), axis=0, keepdims=True)

    place = place_ref[...]
    place = lax.rem(place, NSEG) * Q_DEV + lax.div(place, NSEG)
    at_rank = lax.broadcasted_iota(jnp.int32, (FIELD, tiles), 0).astype(f32) == rank
    fields = [
        jnp.where(at_rank, jnp.broadcast_to(f.astype(f32), at_rank.shape), 0.0)
        for f in (place, kind_ref[...], len_ref[...])
    ]
    fields = jnp.concatenate(fields + [jnp.zeros((FIELD, tiles), f32)], axis=0).astype(bf16)
    meta[...] = dot(goes_bf, fields, 1)

    def lay_meta(i, carry):
        meta_send[i] = meta[pl.ds(i, 1), :]
        return carry

    lax.fori_loop(0, owners, lay_meta, 0)
    meta_recv[0] = meta_send[0]

    loads[5].wait()
    wide[...] = pix_ref[...].astype(f32)
    lengths = len_ref[...].astype(f32)
    lengths = jnp.concatenate(
        [
            jnp.transpose(jnp.broadcast_to(lengths[:, i : i + TP], (TP, TP)))
            for i in range(0, tiles, TP)
        ],
        axis=0,
    )
    live = lax.broadcasted_iota(jnp.int32, (tiles, TP), 1).astype(f32) < lengths
    masked = jnp.concatenate(
        [
            jnp.where(live, wide[pl.ds(s, tiles, stride=shots), :], 0.0).astype(bf16)
            for s in range(shots)
        ],
        axis=1,
    )

    def meta_copy(here, i):
        return pltpu.make_async_remote_copy(
            src_ref=meta_send.at[here], dst_ref=meta_recv.at[here],
            send_sem=meta_send_sem, recv_sem=meta_recv_sem,
            device_id=(block, lax.bitwise_xor(me, i)), device_id_type=MESH,
        )

    def pixel_copy(here, part, sem, i):
        return pltpu.make_async_remote_copy(
            src_ref=send.at[here, part], dst_ref=recv.at[here, part],
            send_sem=send_sem, recv_sem=sem,
            device_id=(block, lax.bitwise_xor(me, i)), device_id_type=MESH,
        )

    def group_of(k):
        return sum(k >= start for start in STARTS[1:-1])

    third = rows // 3
    pieces = [pl.ds(part * third, third) for part in range(3)]

    def pack(first, count):
        spot = lax.broadcasted_iota(jnp.int32, (count * cap, tiles), 0) + first * cap
        placing = (spot.astype(f32) == position).astype(f32).astype(bf16)
        packed = dot(placing, masked)
        for d in range(count):
            mine = packed[d * cap : (d + 1) * cap]
            mine = jnp.concatenate([mine[:, s * TP : (s + 1) * TP] for s in range(shots)], axis=0)
            send[first + d] = mine.astype(bf16)

    for first in range(0, owners, BATCH):
        pack(first, BATCH)
    recv[0] = send[0]

    pl.semaphore_wait(barrier, owners)
    for k in range(1, owners):
        meta_copy(k, order[k]).start()
    for part in range(2):
        for k in range(1, owners):
            pixel_copy(k, pieces[part], piece_sem.at[part], order[k]).start()

    others = pl.ds(1, owners - 1)
    for load in loads[6:10]:
        load.wait()
    meta_copy(others, 1).wait_recv()

    for k in range(1, owners):
        pixel_copy(k, pieces[2], piece_sem.at[2 + group_of(k)], order[k]).start()

    entries = dot(source_ref[...], meta_recv[...].reshape(owners, TP).astype(bf16))
    fields_col[...] = dot((entries * entry_ref[...]).astype(bf16), spread_ref[...])
    slots = Q_DEV * NSEG
    slot = lax.broadcasted_iota(jnp.int32, (slots, TP), 0).astype(f32)
    for i in range(owners * cap // TP):
        line = jnp.transpose(fields_col[i * TP : (i + 1) * TP, :TP])
        line = jnp.broadcast_to(line[0:1], (slots, TP))
        chosen[:, i * TP : (i + 1) * TP] = (slot == line).astype(f32).astype(bf16)

    kinds = weights_ref.shape[0]
    weights = weights_ref[...].reshape(kinds * TP, TP)

    def mark_kinds(i, carry):
        kind = fields_col[pl.ds(pl.multiple_of(i * cap, 8), cap), TP : 2 * TP]
        is_kind[i] = jnp.concatenate([kind] * shots, axis=0).astype(bf16)
        return carry

    def keep(here, column, product):
        hi, lo = split(product)
        values[here, 2 * column * TP : (2 * column + 1) * TP] = hi
        values[here, (2 * column + 1) * TP : (2 * column + 2) * TP] = lo

    def interpolate(first, count, start, end, first_shot, last_shot):
        here = pl.ds(pl.multiple_of(first * cap, 16), count * cap)
        size, these = end - start, pl.ds(first, count)
        pixels = recv[these, start:end].reshape(count * size, TP)
        kind = is_kind[these, start:end].reshape(count * size, TP)
        none = jnp.zeros_like(pixels)
        spread = [jnp.where(kind == jnp.asarray(k, bf16), pixels, none) for k in range(kinds)]
        product = dot(jnp.concatenate(spread, axis=1), weights)
        for s in range(first_shot, last_shot):
            mine = [
                product[i * size + s * cap - start : i * size + (s + 1) * cap - start]
                for i in range(count)
            ]
            keep(here, s, jnp.concatenate(mine, axis=0))

    def interpolate_live(g, carry):
        span = BATCH * cap
        here = pl.ds(pl.multiple_of(g * span, 16), span)
        pixel = lax.broadcasted_iota(jnp.int32, (span, TP), 1).astype(f32)
        kind = fields_col[here, TP : 2 * TP]
        alive = jnp.where(pixel < fields_col[here, 2 * TP :], kind, -1.0)
        spread = [(alive == float(k)).astype(f32).astype(bf16) for k in range(kinds)]
        keep(here, shots, dot(jnp.concatenate(spread, axis=1), weights))
        return carry

    lax.fori_loop(0, owners // BATCH, interpolate_live, 0)
    lax.fori_loop(0, owners, mark_kinds, 0)

    def gather(s, target, start=0, end=owners * cap):
        both = dot(chosen[:, start:end], values[start:end, 2 * s * TP : (2 * s + 2) * TP])
        both = both[:, :TP] + both[:, TP:]
        cycles[target] = both + cycles[target] if start else both

    gather(shots, mask)

    def put(here, real, imag):
        for j, part in enumerate((real, imag)):
            hi, lo = split(part)
            high[here, j * TP : (j + 1) * TP] = hi
            low[here, j * TP : (j + 1) * TP] = lo

    def band(s, k):
        return pl.ds(pl.multiple_of(s * ROWS + k * Q_DEV, 16), Q_DEV)

    def forward(s):
        x = [cycles[s, a * Q_DEV : (a + 1) * Q_DEV, :] for a in range(NSEG)]
        total = [None] + [x[a] + x[NSEG - a] for a in range(1, HALF)]
        differ = [None] + [x[a] - x[NSEG - a] for a in range(1, HALF)]
        real = cosine_sums(x[0], x[HALF], total)
        imag = sine_sums(differ)
        for k in range(FREQS):
            here = band(s, k)
            cos, sin = turns_ref[0, k : k + 1, :], turns_ref[1, k : k + 1, :]
            if k == 0:
                put(here, real[k], jnp.zeros_like(real[k]))
            elif k == HALF:
                put(here, real[k] * cos, real[k] * sin)
            else:
                put(here, real[k] * cos + imag[k] * sin, real[k] * sin - imag[k] * cos)

    def transform(result, target, first, count):
        here = pl.ds(first * ROWS, count * ROWS)
        hi, lo = high[here, :], low[here, :]
        found = dot(jnp.concatenate([hi, lo, hi], axis=1), dft_ref[...])
        result[pl.ds(target * ROWS, count * ROWS), :] = found

    def correlate(s, following, target):
        for k in range(FREQS):
            mine = spectra[band(s, k), :]
            xr, xi = mine[:, :TP], mine[:, TP:]
            if following is None:
                put(band(target, k), xr * xr + xi * xi, jnp.zeros_like(xr))
            else:
                differ = mine - spectra[band(following, k), :]
                dr, di = differ[:, :TP], differ[:, TP:]
                put(band(target, k), xr * dr + xi * di, xr * di - xi * dr)

    def back(s):
        parts = []
        for k in range(FREQS):
            here = band(s, k)
            re, im = inverse[here, :TP], inverse[here, TP:]
            cos, sin = turns_ref[2, k : k + 1, :], turns_ref[3, k : k + 1, :]
            parts.append((re * cos - im * sin, re * sin + im * cos))
        sums = cosine_sums(parts[0][0], parts[HALF][0], [p[0] for p in parts])
        turned = sine_sums([p[1] for p in parts])
        found = [None] * NSEG
        found[0], found[HALF] = sums[0], sums[HALF]
        for a in range(1, HALF):
            found[a], found[NSEG - a] = sums[a] + turned[a], sums[a] - turned[a]
        return found

    for load in loads[10:]:
        load.wait()
    forward(mask)
    transform(spectra, mask, mask, 1)
    correlate(mask, None, turned_back + shots)
    transform(inverse, shots, turned_back + shots, 1)
    overlap = back(shots)
    floor = jnp.maximum(0.01 * overlap[0][:, 0:1], 1.0)
    for a in range(NSEG):
        shares[a * Q_DEV : (a + 1) * Q_DEV, :] = 1.0 / jnp.maximum(overlap[a], floor)

    def finish(s):
        found = back(s)
        for a in range(NSEG):
            share = shares[a * Q_DEV : (a + 1) * Q_DEV, :]
            out_ref[s, :, a * TP : (a + 1) * TP] = found[a] * share

    pixel_copy(others, pieces[0], piece_sem.at[0], 1).wait_recv()
    for first in range(0, owners, BATCH):
        interpolate(first, BATCH, 0, third, 0, 1)
    gather(0, 0)
    halo_copy = pltpu.make_async_remote_copy(
        src_ref=cycles.at[0], dst_ref=cycles.at[halo],
        send_sem=halo_sem.at[0], recv_sem=halo_sem.at[1],
        device_id=(left, me), device_id_type=MESH,
    )
    halo_copy.start()
    forward(0)
    transform(spectra, 0, 0, 1)

    pixel_copy(others, pieces[1], piece_sem.at[1], 1).wait_recv()
    for first in range(0, owners, BATCH):
        interpolate(first, BATCH, 16, 48, 1, 2)
    gather(1, 1)
    forward(1)
    transform(spectra, 1, 1, 1)
    correlate(0, 1, turned_back)
    transform(inverse, 0, turned_back, 1)
    finish(0)

    def take_group(g):
        skip = 1 if g == 0 else 0
        pixel_copy(
            pl.ds(STARTS[g] + skip, STARTS[g + 1] - STARTS[g] - skip),
            pieces[2],
            piece_sem.at[2 + g],
            1,
        ).wait_recv()
        interpolate(STARTS[g], STARTS[g + 1] - STARTS[g], 48, rows, 2, shots)

    groups = len(STARTS) - 1
    early = STARTS[groups - LATE] * cap
    for g in range(groups - LATE):
        take_group(g)
    for s in range(2, shots):
        gather(s, s, 0, early)
    for g in range(groups - LATE, groups):
        take_group(g)
    for s in range(2, shots):
        gather(s, s, early, owners * cap)
        forward(s)
    halo_copy.wait_recv()
    forward(halo)
    for s in range(2, shots + 1):
        transform(spectra, s, s, 1)
    for s in range(1, shots):
        correlate(s, s + 1, turned_back + s)
        transform(inverse, s, turned_back + s, 1)
    for s in range(1, shots):
        finish(s)

    halo_copy.wait_send()
    meta_copy(others, 1).wait_send()
    pixel_copy(others, pl.ds(0, rows), piece_sem.at[0], 1).wait_send()


def per_device(intensities, tile_owner, tile_place, tile_kernel, mask_len, interp_weights):
    owners, shot_blocks = lax.axis_size("blk"), lax.axis_size("shot")
    tiles, shots, _ = intensities.shape
    cap = 3 * tiles // owners
    dft, turns = dft_tables()
    order, source, entry, spread = layout_tables(owners, cap, tiles)
    bf16, f32 = jnp.bfloat16, jnp.float32
    slots = Q_DEV * NSEG
    operands = (
        tile_owner.reshape(1, tiles),
        tile_place.reshape(1, tiles),
        tile_kernel.reshape(1, tiles),
        mask_len.reshape(1, tiles),
        jnp.asarray(order),
        intensities.reshape(tiles * shots, TP),
        jnp.asarray(source),
        jnp.asarray(entry),
        jnp.asarray(spread),
        interp_weights,
        jnp.asarray(turns),
        jnp.asarray(dft),
    )
    return pl.pallas_call(
        functools.partial(kernel, owners, cap, shots, shot_blocks, len(operands)),
        out_shape=jax.ShapeDtypeStruct((shots, Q_DEV, ANG), f32),
        in_specs=[pl.BlockSpec(memory_space=pltpu.HBM)] * len(operands),
        out_specs=pl.BlockSpec(memory_space=pltpu.VMEM),
        scratch_shapes=[pltpu.VMEM(x.shape, x.dtype) for x in operands]
        + [pltpu.SemaphoreType.DMA((len(operands),))]
        + [
            pltpu.VMEM((tiles * shots, TP), f32),
            pltpu.VMEM((owners, cap * shots, TP), bf16),
            pltpu.VMEM((owners, cap * shots, TP), bf16),
            pltpu.VMEM((owners, TP), f32),
            pltpu.VMEM((owners, 1, TP), f32),
            pltpu.VMEM((owners, 1, TP), f32),
            pltpu.VMEM((owners * cap, 3 * TP), f32),
            pltpu.VMEM((owners, cap * shots, TP), bf16),
            pltpu.VMEM((slots, owners * cap), bf16),
            pltpu.VMEM((owners * cap, (shots + 1) * 2 * TP), bf16),
            pltpu.VMEM((shots + 2, slots, TP), f32),
            pltpu.VMEM((slots, TP), f32),
            pltpu.VMEM(((2 * shots + 3) * ROWS, 2 * TP), bf16),
            pltpu.VMEM(((2 * shots + 3) * ROWS, 2 * TP), bf16),
            pltpu.VMEM(((shots + 2) * ROWS, 2 * TP), f32),
            pltpu.VMEM(((shots + 1) * ROWS, 2 * TP), f32),
            pltpu.SemaphoreType.DMA,
            pltpu.SemaphoreType.DMA((len(STARTS) + 1,)),
            pltpu.SemaphoreType.DMA,
            pltpu.SemaphoreType.DMA,
            pltpu.SemaphoreType.DMA((2,)),
        ],
        compiler_params=pltpu.CompilerParams(
            collective_id=0, has_side_effects=True, vmem_limit_bytes=40 * 2**20
        ),
        cost_estimate=pl.CostEstimate(
            flops=3 * 10**9, bytes_accessed=2 * 10**6, transcendentals=0
        ),
    )(*(pltpu.with_memory_space_constraint(x, pltpu.HBM) for x in operands))


def solution(mesh):
    placed = (P("blk", "shot", None), P("blk"), P("blk"), P("blk"), P("blk"), P())
    return jax.shard_map(
        per_device, mesh=mesh, in_specs=placed, out_specs=P("shot", "blk", None), check_vma=False
    )
```
